128 devices in a mesh: bx: 16 (over y, x_hi, core), by: 8 (over z, x_lo).
Axes of the slice: x: 4 (x_hi: 2, x_lo: 2; x = x_hi * 2 + x_lo), y: 4, z: 4, core: 2. Of those that a mesh axis runs over, the one named last changes fastest.
Arguments:
- fields: float32 [4, 512, 1024, 128], P(None, 'bx', 'by'), may hold values from -6 to 6
- ground: int32 [512, 1024], P('bx', 'by'), may hold values 0 or 1
- observers: float32 [3, 131072], P(None, 'bx'), may hold values from -1 to 1
- slots: int32 [131072], P('bx'), may hold values from 0 to 62
- fractions: float32 [131072], P('bx'), may hold values from 0 to 1
- owners: int32 [131072, 1], P('bx'), may hold values from 0 to 127; in each aligned block of 8192 rows (0 to 8191, 8192 to 16383, ...) at most 128 rows name the same one
- arrival_cell: int32 [128, 16, 128], P(('bx', 'by')), may hold values from 0 to 524287
- panel_points: float32 [3, 16384], P(None, 'by'), may hold values from -1 to 1
- panel_normals: float32 [3, 16384], P(None, 'by'), may hold values from -4 to 4
- sources: bfloat16 [3, 16384, 64], P(None, 'by'), may hold values from -0.02734375 to 0.02734375
Outputs:
- new_fields: float32 [4, 512, 1024, 128], P(None, 'bx', 'by')
The draws below stay inside these ranges and needn't reach their ends.
Inputs may be any that keep to these rules, and one draw needn't show every extreme that they name: `owners`: observers are in blocks of 8192 consecutive rows, one block a bx index; within a block no device is named by more than 128 observers, and that most is reached. Device numbers are bx index * 8 + by index. `arrival_cell`: cells are numbered (x * 128 + y) * 128 + z inside a brick; entries past an owner's count for a block are never used.
All inputs are finite; a program needn't handle non-finite values. No bound on the sum of `ground` on one device may be relied on, other than what follows from the above.
Results may differ from the reference program's by a relative error of at most 0.0003.
Values sent between devices are 32-bit elements; how exact they have to be, the bound alone decides.
A program may use at most 128 MiB of HBM per device.

```python
import math
import jax
import jax.numpy as jnp
import numpy as np
from jax import lax

GX = 32
GY = 128
GZ = 128
STEPS = 2
M_DEV = 8192
P_DEV = 2048
TS = 64
NX = 512
NY = 1024
M = 131072
P_SIZE = 16384
CAP = 128
N_BX = 16
N_BY = 8
DEVICES = 128


def with_ends(drawn, stream_key, least, largest):
    longest = drawn.shape.index(max(drawn.shape))
    spots = []
    for shift in (0, 1):
        where = [jax.random.randint(jax.random.fold_in(stream_key, axis), (), 0, length) for axis, length in enumerate(drawn.shape)]
        where[longest] = (where[longest] + shift) % drawn.shape[longest]
        spots.append(tuple(where))
    return drawn.at[spots[0]].set(least).at[spots[1]].set(largest)


def steps_of(rng, extent, cuts, low, top_value):
    def one(axis_at, blocks):
        heights = jax.random.uniform(jax.random.fold_in(jax.random.fold_in(rng, 6), axis_at), (blocks,), jnp.float32, low / len(cuts), top_value / len(cuts))
        return jnp.repeat(jnp.exp(heights), extent[axis_at] // blocks).reshape((-1,) + (1,) * (len(extent) - axis_at - 1))

    loudness = one(*cuts[0])
    for cut in cuts[1:]:
        loudness = loudness * one(*cut)
    return loudness


def shared_out(rng, own, number, rows, number_of, top, limit, skew):
    order = jax.random.permutation(rng, number_of)
    heavy_load, usual = portions_of(number_of, rows * top, limit, skew, True), portions_of(number_of, rows * top, limit, skew, False)
    places = jnp.arange(number_of)

    def named(sizes, rotation):
        used = int((sizes > 0).sum())
        fixed = max(1, used // 4)
        passed = fixed + (places - fixed + rotation * (used - fixed)) % max(1, number_of - fixed)
        return jnp.zeros((number_of,), jnp.int32).at[order[jnp.where(places < fixed, places, passed)]].set(jnp.asarray(sizes, jnp.int32))

    sizes = jnp.where(number % 4 == 0, named(heavy_load, number // 4), named(usual, number - number // 4 - 1))
    mixed = jax.random.permutation(jax.random.fold_in(own, 3), number_of)
    giver, taker = mixed[0:number_of // 2 * 2:2], mixed[1:number_of // 2 * 2:2]
    margin = jnp.minimum(sizes[giver] - 1, limit - sizes[taker]) // 2
    margin = jnp.where((giver == order[0]) | (taker == order[0]) | (sizes[taker] == 0), 0, jnp.maximum(margin, 0))
    passed = jax.random.randint(jax.random.fold_in(own, 4), (number_of // 2,), 0, 1 << 20) % (margin + 1)
    sizes = sizes.at[giver].add(-passed).at[taker].add(passed)
    labels = jnp.searchsorted(jnp.cumsum(sizes), jnp.arange(rows * top), side="right").astype(jnp.int32)
    listing = labels.reshape(top, rows).T
    listing = listing[jax.random.permutation(jax.random.fold_in(own, 1), rows)]
    rotation = jax.random.randint(jax.random.fold_in(own, 2), (rows, 1), 0, top)
    return jnp.take_along_axis(listing, (jnp.arange(top)[None, :] + rotation) % top, axis=1)


def portions_of(number_of, total, reach, skew, full):
    weights = [(1 << 20) // math.isqrt(grade ** skew) + 1 for grade in range(1, number_of + 1)]
    largest = reach if full else min(reach, max(-(-total // number_of), total * weights[0] // sum(weights)))
    least = 1 if total - largest >= number_of - 1 else 0
    holding, surplus = [largest] + [least] * (number_of - 1), total - largest - least * (number_of - 1)
    while surplus > 0:
        movable = [i for i in range(1, number_of) if holding[i] < largest] or [i for i in range(1, number_of) if holding[i] < reach]
        whole, left = sum([weights[i] for i in movable]), surplus
        for i in movable:
            addition = min(reach - holding[i], max(1, left * weights[i] // whole), surplus)
            holding[i] = holding[i] + addition
            surplus = surplus - addition
    return np.array(holding)


def scatter_about(stream_key, dims, spread, reach, split=(), kind=jnp.bfloat16):
    values = spread * jax.random.normal(stream_key, dims, jnp.float32)
    if split:
        values = values * steps_of(stream_key, dims, split, -0.22, 0.18)
    return jnp.clip(values, -reach, reach).astype(kind)


def setup_inputs(seed: int = 0) -> dict:
    arg_keys = jax.random.split(jax.random.key(seed), 11)
    fields = scatter_about(arg_keys[0], (4, NX, NY, GZ), 1.0, 6.0, ((1, 16), (2, 8)), jnp.float32)
    ground = with_ends((jax.random.randint(arg_keys[1], (NX, NY), 0, 4) < 3).astype(jnp.int32), jax.random.fold_in(arg_keys[1], 1), 0, 1)
    observers = jnp.clip(jax.random.uniform(arg_keys[2], (3, M), jnp.float32, -1.0, 1.0) * steps_of(arg_keys[2], (3, M), ((1, 16),), -0.4, 0.0), -1.0, 1.0)
    slots = with_ends(jax.random.randint(arg_keys[3], (M,), 0, TS - 1), jax.random.fold_in(arg_keys[3], 1), 0, (TS - 1) - 1).astype(jnp.int32)
    fractions = jnp.clip(1.0 * jax.random.uniform(arg_keys[4], (M,), jnp.float32) ** steps_of(arg_keys[4], (M,), ((0, 16),), -0.2, 0.2), 0.0, 1.0)
    owners_keys = jax.random.split(jax.random.fold_in(arg_keys[5], 1), M // M_DEV)
    owners_turns = jax.random.permutation(jax.random.fold_in(arg_keys[5], 3), M // M_DEV)
    owners = jax.vmap(lambda own, number: shared_out(jax.random.fold_in(arg_keys[5], 2), own, number, M_DEV, DEVICES, 1, CAP, 1))(owners_keys, owners_turns).reshape((M, 1))
    arrival_cell = with_ends(jax.random.randint(arg_keys[6], (DEVICES, N_BX, CAP), 0, GX * GY * GZ), jax.random.fold_in(arg_keys[6], 1), 0, (GX * GY * GZ) - 1).astype(jnp.int32)
    panel_points = jnp.clip(jax.random.uniform(arg_keys[7], (3, P_SIZE), jnp.float32, -1.0, 1.0) * steps_of(arg_keys[7], (3, P_SIZE), ((1, 8),), -0.4, 0.0), -1.0, 1.0)
    panel_normals = scatter_about(arg_keys[8], (3, P_SIZE), 1.0, 4.0, ((1, 8),), jnp.float32)
    sources = scatter_about(arg_keys[9], (3, P_SIZE, TS), (3 * P_DEV * N_BY) ** -0.5, 0.02734375, ((1, 8),))
    return {"fields": fields, "ground": ground, "observers": observers, "slots": slots, "fractions": fractions, "owners": owners, "arrival_cell": arrival_cell, "panel_points": panel_points, "panel_normals": panel_normals, "sources": sources}


STENCIL_WEIGHTS = (0.770882380518, -0.166705904415, 0.02084314277)
TIME_STEP = 0.5
SOFTENING = 0.01

def centered(grid_field, axis):
    inner_size = grid_field.shape[axis] - 6
    summed = jnp.zeros_like(lax.slice_in_dim(grid_field, 3, 3 + inner_size, axis=axis))
    for offset, weight in enumerate(STENCIL_WEIGHTS, 1):
        forward = lax.slice_in_dim(grid_field, 3 + offset, 3 + offset + inner_size, axis=axis)
        behind = lax.slice_in_dim(grid_field, 3 - offset, 3 - offset + inner_size, axis=axis)
        summed = summed + weight * (forward - behind)
    return summed

def ground_pad(grid_field, ground_flags, parity):
    mirror_cells = parity * ground_flags[:, :, None] * grid_field[:, :, 2::-1]
    top_cells = jnp.zeros(grid_field.shape[:2] + (3,), jnp.float32)
    return jnp.concatenate([mirror_cells, grid_field, top_cells], axis=2)

def velocity_update(pressure_wide, velocity, ground_flags):
    pressure_core = pressure_wide[3:-3, 3:-3]
    grad_x = centered(pressure_wide[:, 3:-3], 0)
    grad_y = centered(pressure_wide[3:-3, :], 1)
    grad_z = centered(ground_pad(pressure_core, ground_flags, 1.0), 2)
    return velocity - TIME_STEP * jnp.stack([grad_x, grad_y, grad_z])

def pressure_update(velocity_wide, pressure, ground_flags):
    div_x = centered(velocity_wide[0][:, 3:-3], 0)
    div_y = centered(velocity_wide[1][3:-3, :], 1)
    div_z = centered(ground_pad(velocity_wide[2][3:-3, 3:-3], ground_flags, -1.0), 2)
    return pressure - TIME_STEP * (div_x + div_y + div_z)

def panel_kernel(points, panel_points, panel_normals):
    offset = points[:, :, None] - panel_points[:, None, :]
    distance_sq = lax.optimization_barrier(jnp.sum(offset * offset, axis=0)) + SOFTENING
    inverse = 1.0 / jnp.sqrt(distance_sq)
    normal_part = lax.optimization_barrier(jnp.sum(offset * panel_normals[:, None, :], axis=0))
    near_field = normal_part * inverse * inverse
    return jnp.concatenate([inverse, near_field, near_field * inverse], axis=1).astype(jnp.bfloat16)

def observed_values(points, slot_rows, fraction_rows, panel_points, panel_normals, source_matrix):
    kernel = panel_kernel(points, panel_points, panel_normals)
    history = jnp.dot(kernel, source_matrix, preferred_element_type=jnp.float32)
    sample_ids = jnp.arange(history.shape[1], dtype=jnp.int32)[None, :]
    weights = jnp.where(sample_ids == slot_rows[:, None], 1.0 - fraction_rows[:, None], 0.0)
    weights = weights + jnp.where(sample_ids == slot_rows[:, None] + 1, fraction_rows[:, None], 0.0)
    return lax.optimization_barrier(jnp.sum(history * weights, axis=1))

def reference(fields, ground, observers, slots, fractions, owners, arrival_cell, panel_points, panel_normals, sources):
    total_rows = observers.shape[1]
    block_rows = min(512, M_DEV)
    source_matrix = sources.reshape(-1, sources.shape[2])

    def one_block(block_id):
        row_start = block_id * block_rows
        points = lax.dynamic_slice_in_dim(observers, row_start, block_rows, 1)
        slot_rows = lax.dynamic_slice_in_dim(slots, row_start, block_rows, 0)
        fraction_rows = lax.dynamic_slice_in_dim(fractions, row_start, block_rows, 0)
        return observed_values(points, slot_rows, fraction_rows, panel_points, panel_normals, source_matrix)
    values = lax.map(one_block, jnp.arange(total_rows // block_rows, dtype=jnp.int32)).reshape(-1)
    devices = N_BX * N_BY
    target = owners[:, 0]

    def ranks_of(owner_rows):
        onehot = (owner_rows[:, None] == jnp.arange(devices, dtype=jnp.int32)[None, :]).astype(jnp.int32)
        return lax.optimization_barrier(jnp.sum(jnp.cumsum(onehot, axis=0) * onehot, axis=1)) - 1
    slot_rank = lax.map(ranks_of, target.reshape(N_BX, M_DEV)).reshape(-1)
    blocks = jnp.arange(total_rows, dtype=jnp.int32) // M_DEV
    cell_ids = arrival_cell[target, blocks, slot_rank]
    pos_x = target // N_BY * GX + cell_ids // (GY * GZ)
    pos_y = target % N_BY * GY + cell_ids // GZ % GY
    pos_z = cell_ids % GZ
    pressure = fields[0].at[pos_x, pos_y, pos_z].add(values)
    velocity = fields[1:]
    ground_flags = ground.astype(jnp.float32)
    for _ in range(STEPS):
        pressure_wide = jnp.pad(pressure, ((3, 3), (3, 3), (0, 0)))
        velocity = velocity_update(pressure_wide, velocity, ground_flags)
        velocity_wide = jnp.pad(velocity, ((0, 0), (3, 3), (3, 3), (0, 0)))
        pressure = pressure_update(velocity_wide, pressure, ground_flags)
    return jnp.concatenate([pressure[None], velocity], axis=0)
```

```python
import functools

import jax
import jax.numpy as jnp
from jax import lax
from jax.experimental import pallas as pl
from jax.experimental.pallas import tpu as pltpu
from jax.sharding import PartitionSpec as P

BF = jnp.bfloat16
F32 = jnp.float32
MESH = pl.DeviceIdType.MESH
WEIGHTS = (0.770882380518, -0.166705904415, 0.02084314277)
DT = 0.5
SOFTENING = 0.01
REACH = 3
WIDE = 6
PAD = 8
FEATURES = 80
MERGE = False


def split3(x):
    a = x.astype(BF).astype(F32)
    r = x - a
    b = r.astype(BF).astype(F32)
    return a, b, r - b


def dot(a, b):
    return jnp.dot(a, b, preferred_element_type=F32)


def dot_nt(a, b):
    return lax.dot_general(a, b, (((1,), (1,)), ((), ())), preferred_element_type=F32)


def panel_scratch(m, q, devices):
    return [
        pltpu.VMEM((8, m), F32),
        pltpu.VMEM((8, q), F32),
        pltpu.VMEM((2, q, FEATURES), BF),
        pltpu.VMEM((3 * devices, 128), F32),
        pltpu.VMEM((devices, 128), F32),
    ]


def panel_part(nbx, nby, obs, slots, fracs, owners, pts, nrm, src, packet, eo, ep, feat, pieces, base):
    m = obs.shape[1]
    q = pts.shape[1]
    samples = src.shape[1]
    devices = nbx * nby
    tile = min(1024, m)
    chunk = min(512, q)
    sub = 256

    o = obs[...]
    eo[0:3, :] = o
    eo[3:4, :] = jnp.sum(o * o, axis=0, keepdims=True)
    eo[4:5, :] = jnp.ones((1, m), F32)
    eo[5:8, :] = jnp.zeros((3, m), F32)
    p = pts[...]
    n = nrm[...]

    def lay(k):
        s = split3(ep[...])
        rows = [s[0], s[1], s[2]] * 3 + [jnp.zeros_like(s[0])]
        table = jnp.concatenate(rows + [jnp.zeros((128 - FEATURES, q), F32)], axis=0)
        feat[k] = table.T[:, :FEATURES].astype(BF)

    ep[0:3, :] = -2.0 * p
    ep[3:4, :] = jnp.ones((1, q), F32)
    ep[4:5, :] = jnp.sum(p * p, axis=0, keepdims=True) + SOFTENING
    ep[5:8, :] = jnp.zeros((3, q), F32)
    lay(0)
    ep[0:3, :] = n
    ep[3:4, :] = jnp.zeros((1, q), F32)
    ep[4:5, :] = -jnp.sum(p * n, axis=0, keepdims=True)
    lay(1)
    pieces[...] = jnp.zeros_like(pieces)
    base[...] = jnp.zeros_like(base)
    row = lax.broadcasted_iota(jnp.int32, (devices, 1), 0)
    row_owner = (row % nbx) * nby + row // nbx
    before = (
        lax.broadcasted_iota(jnp.int32, (sub, sub), 0) < lax.broadcasted_iota(jnp.int32, (sub, sub), 1)
    ).astype(F32).astype(BF)
    ranks = lax.broadcasted_iota(jnp.int32, (128, 1), 0).astype(F32)
    times = lax.broadcasted_iota(jnp.int32, (samples, 1), 0)

    def one_tile(t, carry):
        o0 = pl.multiple_of(t * tile, tile)
        here = pl.ds(o0, tile)
        e = split3(eo[:, here])
        of = jnp.concatenate(
            [e[0]] * 3 + [e[1]] * 3 + [e[2]] * 3 + [jnp.zeros_like(e[0])], axis=0
        ).astype(BF)

        def one_chunk(c, acc):
            q0 = pl.multiple_of(c * chunk, chunk)
            rows = pl.ds(q0, chunk)
            inverse = lax.rsqrt(dot(feat[0, rows, :], of))
            near = dot(feat[1, rows, :], of) * inverse * inverse
            far = near * inverse
            acc = acc + dot(src[0, :, rows], inverse.astype(BF))
            acc = acc + dot(src[1, :, rows], near.astype(BF))
            return acc + dot(src[2, :, rows], far.astype(BF))

        history = lax.fori_loop(0, q // chunk, one_chunk, jnp.zeros((samples, tile), F32))
        slot = slots[:, here]
        frac = fracs[:, here]
        weights = jnp.where(times == slot, 1.0 - frac, 0.0) + jnp.where(times == slot + 1, frac, 0.0)
        value = jnp.sum(history * weights, axis=0, keepdims=True)
        parts = split3(value)
        owner = owners[:, here]
        for s in range(tile // sub):
            cut = slice(s * sub, (s + 1) * sub)
            mine = owner[:, cut] == row_owner
            hot = jnp.where(mine, 1.0, 0.0)
            earlier = dot(hot.astype(BF), before) + base[:, 0:1]
            rank = jnp.sum(hot * earlier, axis=0, keepdims=True)
            base[...] += jnp.sum(hot, axis=1, keepdims=True)
            at_rank = jnp.where(rank == ranks, 1.0, 0.0).astype(BF)
            loads = jnp.concatenate([jnp.where(mine, v[:, cut], 0.0) for v in parts], axis=0).astype(BF)
            pieces[...] += dot_nt(loads, at_rank)
        return carry

    lax.fori_loop(0, m // tile, one_tile, 0)
    packet[...] = pieces[0:devices, :] + pieces[devices:2 * devices, :] + pieces[2 * devices:, :]


def panel_kernel(nbx, nby, *refs):
    panel_part(nbx, nby, *refs)


def box_kernel(nbx, nby, packet, cells, ground, fields, out, pa, pb, us, vs, ws, flags, zmat, hot_own, hot_lr, hot_du, bt,
               gathered, agg, arrived, passed, passed_cells, load_sem, raw_send, raw_recv, one_send, one_recv,
               two_send, two_recv, nb_send, nb_recv, rim_send, rim_recv, out_sem):
    bx = lax.axis_index("bx")
    by = lax.axis_index("by")
    gx, gy, gz = fields.shape[1:]
    arrivals = nbx * 128
    has = (bx > 0, bx < nbx - 1, by > 0, by < nby - 1)
    to = (
        (jnp.maximum(bx - 1, 0), by),
        (jnp.minimum(bx + 1, nbx - 1), by),
        (bx, jnp.maximum(by - 1, 0)),
        (bx, jnp.minimum(by + 1, nby - 1)),
    )
    back = (1, 0, 3, 2)

    barrier = pltpu.get_barrier_semaphore()
    for i in range(1, nby):
        pl.semaphore_signal(barrier, inc=1, device_id=(bx, lax.rem(by + i, nby)), device_id_type=MESH)
    for i in range(1, nbx):
        pl.semaphore_signal(barrier, inc=1, device_id=(lax.rem(bx + i, nbx), by), device_id_type=MESH)
    pl.semaphore_wait(barrier, nby - 1 + nbx - 1)

    def remote(src, dst, send, recv, target):
        return pltpu.make_async_remote_copy(
            src_ref=src, dst_ref=dst, send_sem=send, recv_sem=recv, device_id=target, device_id_type=MESH
        )

    firsts = []
    for i in range(1, nby):
        peer = lax.rem(by + i, nby)
        rows = pl.ds(pl.multiple_of(peer * nbx, nbx), nbx)
        copy = remote(packet.at[rows, :], gathered.at[i], one_send.at[i], one_recv.at[i], (bx, peer))
        copy.start()
        firsts.append(copy)

    x_core = pl.ds(WIDE, gx)
    y_core = pl.ds(PAD, gy)
    give_p = (
        fields.at[0, pl.ds(0, WIDE)],
        fields.at[0, pl.ds(gx - WIDE, WIDE)],
        fields.at[0, :, pl.ds(0, PAD)],
        fields.at[0, :, pl.ds(gy - PAD, PAD)],
    )
    give_v = (
        fields.at[1, pl.ds(0, REACH)],
        fields.at[1, pl.ds(gx - REACH, REACH)],
        fields.at[2, :, pl.ds(0, PAD)],
        fields.at[2, :, pl.ds(gy - PAD, PAD)],
    )

    def rim(ref):
        return (
            ref.at[pl.ds(0, WIDE), y_core],
            ref.at[pl.ds(WIDE + gx, WIDE), y_core],
            ref.at[x_core, pl.ds(0, PAD)],
            ref.at[x_core, pl.ds(PAD + gy, PAD)],
        )

    rim_a = rim(pa)
    rim_b = rim(pb)
    rim_v = (
        us.at[pl.ds(0, REACH)],
        us.at[pl.ds(REACH + gx, REACH)],
        vs.at[:, pl.ds(0, PAD)],
        vs.at[:, pl.ds(PAD + gy, PAD)],
    )

    raw = []
    for s in range(4):
        raw.append((
            remote(cells.at[0], passed_cells.at[back[s]], raw_send.at[s], raw_recv.at[s], to[s]),
            remote(give_p[s], rim_a[back[s]], raw_send.at[4 + s], raw_recv.at[4 + s], to[s]),
            remote(give_v[s], rim_v[back[s]], raw_send.at[8 + s], raw_recv.at[8 + s], to[s]),
        ))

    def landed(src, dst, recv, s):
        return remote(src, dst, raw_send.at[s], recv, to[s % 4])

    for s in range(4):
        @pl.when(has[s])
        def _(s=s):
            for copy in raw[s]:
                copy.start()

    loads = [
        pltpu.make_async_copy(fields.at[0], pa.at[x_core, y_core], load_sem.at[0]),
        pltpu.make_async_copy(fields.at[1], us.at[pl.ds(REACH, gx)], load_sem.at[1]),
        pltpu.make_async_copy(fields.at[2], vs.at[:, y_core], load_sem.at[2]),
        pltpu.make_async_copy(fields.at[3], ws, load_sem.at[3]),
    ]
    for copy in loads:
        copy.start()

    for s in range(4):
        @pl.when(jnp.logical_not(has[s]))
        def _(s=s):
            rim_a[s][...] = jnp.zeros(rim_a[s].shape, F32)
            rim_b[s][...] = jnp.zeros(rim_b[s].shape, F32)
            rim_v[s][...] = jnp.zeros(rim_v[s].shape, F32)

    scaled = [DT * w for w in WEIGHTS]
    source = lax.broadcasted_iota(jnp.int32, (gz, 2 * gz), 0)
    column = lax.broadcasted_iota(jnp.int32, (gz, 2 * gz), 1)
    difference = jnp.zeros((gz, 2 * gz), F32)
    for j, w in enumerate(scaled, 1):
        difference = jnp.where(jnp.logical_and(column < gz, source - column == j), w, difference)
        difference = jnp.where(jnp.logical_and(column < gz, column - source == j), -w, difference)
        difference = jnp.where(jnp.logical_and(column >= gz, source + column - gz + 1 == j), -w, difference)
    coarse = difference.astype(BF)
    zmat[0:gz, :] = coarse
    zmat[gz:2 * gz, :] = coarse
    zmat[2 * gz:, :] = (difference - coarse.astype(F32)).astype(BF)

    ground_t = ground[...].astype(F32).T
    for x in range(gx):
        flags[x] = jnp.broadcast_to(ground_t[:, x:x + 1], (gy, gz))

    def fill(ref, rows, row_id):
        step = min(256, rows)

        def go(i, carry):
            r0 = pl.multiple_of(i * step, step)
            ids = lax.broadcasted_iota(jnp.int32, (step, 1), 0) + r0
            for b in range(nbx):
                ref[pl.ds(r0, step), b * 128:(b + 1) * 128] = jnp.where(
                    ids == row_id[b:b + 1, :], 1.0, 0.0
                ).astype(BF)
            return carry

        lax.fori_loop(0, rows // step, go, 0)

    fill(hot_own, gx * gy, cells[0] // gz)

    for copy in firsts:
        copy.wait_recv()
    mine = pl.ds(pl.multiple_of(by * nbx, nbx), nbx)
    total = packet[mine, :]
    for i in range(1, nby):
        total = total + gathered[i]
    for i in range(nbx):
        agg[i] = total[i:i + 1, :]
    seconds = []
    for i in range(1, nbx):
        peer = lax.rem(bx + i, nbx)
        copy = remote(agg.at[peer], arrived.at[bx], two_send.at[i], two_recv.at[i], (peer, by))
        copy.start()
        seconds.append(copy)
    arrived[bx] = agg[bx]

    cells_in = []
    for s in range(4):
        @pl.when(has[s])
        def _(s=s):
            landed(cells.at[0], passed_cells.at[s], raw_recv.at[back[s]], s).wait_recv()
            row_id = passed_cells[s] // gz
            if s == 0:
                fill(hot_lr.at[0], WIDE * gy, row_id - (gx - WIDE) * gy)
            elif s == 1:
                fill(hot_lr.at[1], WIDE * gy, row_id)
            else:
                y = row_id % gy - (gy - PAD if s == 2 else 0)
                inside = jnp.logical_and(y >= 0, y < PAD)
                fill(hot_du.at[s - 2], gx * PAD, jnp.where(inside, row_id // gy * PAD + y, -1))

    heights = lax.broadcasted_iota(jnp.int32, (gz, 1), 0)

    def targets(values, cell_rows):
        for b in range(nbx):
            v = values(b)
            at = heights == cell_rows[b:b + 1, :] % gz
            hi = v.astype(BF).astype(F32)
            bt[0:gz, b * 128:(b + 1) * 128] = jnp.where(at, hi, 0.0).astype(BF)
            bt[gz:2 * gz, b * 128:(b + 1) * 128] = jnp.where(at, v - hi, 0.0).astype(BF)

    def added(hot):
        both = dot_nt(hot, bt[...])
        return both[:, :gz] + both[:, gz:]

    for copy in seconds:
        copy.wait_recv()
    handed = [
        remote(arrived, passed.at[back[s]], nb_send.at[s], nb_recv.at[s], to[s]) for s in range(4)
    ]
    for s in range(4):
        @pl.when(has[s])
        def _(s=s):
            handed[s].start()

    targets(lambda b: arrived[b], cells[0])
    loads[0].wait()
    planes = 4

    def inject_own(i, carry):
        r0 = pl.multiple_of(i * planes * gy, planes * gy)
        extra = added(hot_own[pl.ds(r0, planes * gy), :]).reshape(planes, gy, gz)
        pa[pl.ds(WIDE + i * planes, planes), PAD:PAD + gy, :] += extra
        return carry

    lax.fori_loop(0, gx // planes, inject_own, 0)

    for s in range(4):
        @pl.when(has[s])
        def _(s=s):
            landed(give_p[s], rim_a[s], raw_recv.at[4 + back[s]], 4 + s).wait_recv()
            landed(give_v[s], rim_v[s], raw_recv.at[8 + back[s]], 8 + s).wait_recv()
            remote(arrived, passed.at[s], nb_send.at[s], nb_recv.at[back[s]], to[s]).wait_recv()
            targets(lambda b: passed[s, b], passed_cells[s])
            if s < 2:
                x0 = 0 if s == 0 else WIDE + gx

                def inject_x(i, carry):
                    r0 = pl.multiple_of(i * gy, gy)
                    pa[x0 + i, PAD:PAD + gy, :] += added(hot_lr[s, pl.ds(r0, gy), :])
                    return carry

                lax.fori_loop(0, WIDE, inject_x, 0)
            else:
                y0 = 0 if s == 2 else PAD + gy
                pa[WIDE:WIDE + gx, y0:y0 + PAD, :] += added(hot_du[s - 2]).reshape(gx, PAD, gz)

    for copy in loads[1:]:
        copy.wait()

    def z_term(f, flag):
        high = f.astype(BF)
        low = (f - high.astype(F32)).astype(BF)
        both = dot(jnp.concatenate([high, low, high], axis=1), zmat[...])
        return both[:, :gz] + flag * both[:, gz:]

    def span(get):
        total = None
        for j, w in enumerate(scaled, 1):
            term = w * (get(j) - get(-j))
            total = term if total is None else total + term
        return total

    def loop(lo, hi, step):
        def go(i, carry):
            step(i)
            return carry

        lax.fori_loop(lo, hi, go, 0)

    def u_plane(p, i):
        us[i] = us[i] - span(lambda j: p[i + REACH + j, PAD:PAD + gy, :])

    def v_rows(p, x, lo, hi):
        vs[x, lo:hi, :] = vs[x, lo:hi, :] - span(lambda j: p[x + WIDE, lo + j:hi + j, :])

    def w_plane(p, x):
        ws[x] = ws[x] - z_term(p[x + WIDE, PAD:PAD + gy, :], flags[x])

    def p_rows(old, new, x, lo, hi):
        change = span(lambda j: us[x + REACH + j, lo:hi, :])
        change = change + span(lambda j: vs[x, PAD + lo + j:PAD + hi + j, :])
        change = change + z_term(ws[x, lo:hi, :], -flags[x, lo:hi, :])
        new[x + WIDE, PAD + lo:PAD + hi, :] = old[x + WIDE, PAD + lo:PAD + hi, :] - change

    def outer_u(p, s):
        lo = 0 if s == 0 else REACH + gx

        @pl.when(has[s])
        def _():
            loop(lo, lo + REACH, lambda i: u_plane(p, i))

    def outer_v(p, s):
        lo = PAD - REACH if s == 2 else PAD + gy

        @pl.when(has[s])
        def _():
            loop(0, gx, lambda x: v_rows(p, x, lo, lo + REACH))

    for s in (0, 1):
        outer_u(pa, s)
    for s in (2, 3):
        outer_v(pa, s)

    def first_velocity(x):
        u_plane(pa, x + REACH)
        v_rows(pa, x, PAD, PAD + gy)
        w_plane(pa, x)

    loop(0, gx, first_velocity)

    give_b = (
        pb.at[pl.ds(WIDE, WIDE), y_core],
        pb.at[pl.ds(gx, WIDE), y_core],
        pb.at[x_core, pl.ds(PAD, PAD)],
        pb.at[x_core, pl.ds(gy, PAD)],
    )
    second_rim = [
        remote(give_b[s], rim_b[back[s]], rim_send.at[s], rim_recv.at[s], to[s]) for s in range(4)
    ]

    def send_rim(s):
        @pl.when(has[s])
        def _():
            second_rim[s].start()

    loop(0, WIDE, lambda x: p_rows(pa, pb, x, 0, gy))
    send_rim(0)
    loop(gx - WIDE, gx, lambda x: p_rows(pa, pb, x, 0, gy))
    send_rim(1)

    def edges(x):
        p_rows(pa, pb, x, 0, PAD)
        p_rows(pa, pb, x, gy - PAD, gy)

    loop(WIDE, gx - WIDE, edges)
    send_rim(2)
    send_rim(3)
    loop(WIDE, gx - WIDE, lambda x: p_rows(pa, pb, x, PAD, gy - PAD))

    def inner_velocity(x):
        v_rows(pb, x, 2 * PAD, gy)
        w_plane(pb, x)

    loop(0, gx, inner_velocity)
    loop(2 * REACH, gx, lambda i: u_plane(pb, i))
    outs = [
        pltpu.make_async_copy(pa.at[x_core, y_core], out.at[0], out_sem.at[0]),
        pltpu.make_async_copy(us.at[pl.ds(REACH, gx)], out.at[1], out_sem.at[1]),
        pltpu.make_async_copy(vs.at[:, y_core], out.at[2], out_sem.at[2]),
        pltpu.make_async_copy(ws, out.at[3], out_sem.at[3]),
    ]
    outs[3].start()
    for s in range(4):
        @pl.when(has[s])
        def _(s=s):
            remote(give_b[s], rim_b[s], rim_send.at[s], rim_recv.at[back[s]], to[s]).wait_recv()
    for s in (0, 1):
        outer_u(pb, s)
    loop(REACH, 2 * REACH, lambda i: u_plane(pb, i))
    loop(gx, gx + REACH, lambda i: u_plane(pb, i))
    outs[1].start()
    for s in (2, 3):
        outer_v(pb, s)

    def outer_rows(x):
        v_rows(pb, x, PAD, 2 * PAD)
        v_rows(pb, x, gy, gy + PAD)

    loop(0, gx, outer_rows)
    outs[2].start()
    loop(0, gx, lambda x: p_rows(pb, pa, x, 0, gy))
    outs[0].start()

    for copy in firsts + seconds:
        copy.wait_send()
    for s in range(4):
        @pl.when(has[s])
        def _(s=s):
            for copy in raw[s]:
                copy.wait_send()
            handed[s].wait_send()
            second_rim[s].wait_send()
    for copy in outs:
        copy.wait()


def vmem():
    return pl.BlockSpec(memory_space=pltpu.VMEM)


def anywhere():
    return pl.BlockSpec(memory_space=pl.ANY)


def body(nbx, nby, fields, ground, observers, slots, fractions, owners, arrival_cell, panel_points, panel_normals,
         sources):
    devices = nbx * nby
    m = observers.shape[1]
    q = panel_points.shape[1]
    gx, gy, gz = fields.shape[1:]
    k = nbx * 128
    packet = pl.pallas_call(
        functools.partial(panel_kernel, nbx, nby),
        out_shape=jax.ShapeDtypeStruct((devices, 128), F32),
        in_specs=[vmem()] * 7,
        out_specs=vmem(),
        scratch_shapes=panel_scratch(m, q, devices),
        compiler_params=pltpu.CompilerParams(vmem_limit_bytes=48 << 20),
        name="panels",
    )(
        observers,
        slots.reshape(1, m),
        fractions.reshape(1, m),
        owners.reshape(1, m),
        panel_points,
        panel_normals,
        sources.transpose(0, 2, 1),
    )
    dma = pltpu.SemaphoreType.DMA
    return pl.pallas_call(
        functools.partial(box_kernel, nbx, nby),
        out_shape=jax.ShapeDtypeStruct(fields.shape, F32),
        in_specs=[vmem(), vmem(), vmem(), anywhere()],
        out_specs=anywhere(),
        scratch_shapes=[
            pltpu.VMEM((gx + 2 * WIDE, gy + 2 * PAD, gz), F32),
            pltpu.VMEM((gx + 2 * WIDE, gy + 2 * PAD, gz), F32),
            pltpu.VMEM((gx + 2 * REACH, gy, gz), F32),
            pltpu.VMEM((gx, gy + 2 * PAD, gz), F32),
            pltpu.VMEM((gx, gy, gz), F32),
            pltpu.VMEM((gx, gy, gz), F32),
            pltpu.VMEM((3 * gz, 2 * gz), BF),
            pltpu.VMEM((gx * gy, k), BF),
            pltpu.VMEM((2, WIDE * gy, k), BF),
            pltpu.VMEM((2, gx * PAD, k), BF),
            pltpu.VMEM((2 * gz, k), BF),
            pltpu.VMEM((nby, nbx, 128), F32),
            pltpu.VMEM((nbx, 1, 128), F32),
            pltpu.VMEM((nbx, 1, 128), F32),
            pltpu.VMEM((4, nbx, 1, 128), F32),
            pltpu.VMEM((4, nbx, 128), jnp.int32),
            dma((4,)),
            dma((12,)),
            dma((12,)),
            dma((nby,)),
            dma((nby,)),
            dma((nbx,)),
            dma((nbx,)),
            dma((4,)),
            dma((4,)),
            dma((4,)),
            dma((4,)),
            dma((4,)),
        ],
        compiler_params=pltpu.CompilerParams(
            collective_id=0, has_side_effects=True, vmem_limit_bytes=56 << 20
        ),
        name="box",
    )(packet, arrival_cell, ground, fields)


def solution(mesh):
    placed = (
        P(None, "bx", "by", None),
        P("bx", "by"),
        P(None, "bx"),
        P("bx"),
        P("bx"),
        P("bx", None),
        P(("bx", "by"), None, None),
        P(None, "by"),
        P(None, "by"),
        P(None, "by", None),
    )
    return jax.shard_map(
        functools.partial(body, mesh.shape["bx"], mesh.shape["by"]),
        mesh=mesh,
        in_specs=placed,
        out_specs=P(None, "bx", "by", None),
        check_vma=False,
    )
```

```python
import functools

import jax
import jax.numpy as jnp
from jax import lax
from jax.experimental import pallas as pl
from jax.experimental.pallas import tpu as pltpu
from jax.sharding import PartitionSpec as P

BF = jnp.bfloat16
F32 = jnp.float32
MESH = pl.DeviceIdType.MESH
WEIGHTS = (0.770882380518, -0.166705904415, 0.02084314277)
DT = 0.5
SOFTENING = 0.01
REACH = 3
WIDE = 6
PAD = 8
FEATURES = 80


def split3(x):
    a = x.astype(BF).astype(F32)
    r = x - a
    b = r.astype(BF).astype(F32)
    return a, b, r - b


def dot(a, b):
    return jnp.dot(a, b, preferred_element_type=F32)


def dot_nt(a, b):
    return lax.dot_general(a, b, (((1,), (1,)), ((), ())), preferred_element_type=F32)


def panel_scratch(m, q, devices):
    return [
        pltpu.VMEM((8, m), F32),
        pltpu.VMEM((8, q), F32),
        pltpu.VMEM((2, q, FEATURES), BF),
        pltpu.VMEM((3 * devices, 128), F32),
        pltpu.VMEM((devices, 128), F32),
    ]


def panel_part(nbx, nby, obs, slots, fracs, owners, pts, nrm, src, packet, eo, ep, feat, pieces, base):
    m = obs.shape[1]
    q = pts.shape[1]
    samples = src.shape[1]
    devices = nbx * nby
    tile = min(1024, m)
    chunk = min(512, q)
    sub = 256

    o = obs[...]
    eo[0:3, :] = o
    eo[3:4, :] = jnp.sum(o * o, axis=0, keepdims=True)
    eo[4:5, :] = jnp.ones((1, m), F32)
    eo[5:8, :] = jnp.zeros((3, m), F32)
    p = pts[...]
    n = nrm[...]

    def lay(k):
        s = split3(ep[...])
        rows = [s[0], s[1], s[2]] * 3 + [jnp.zeros_like(s[0])]
        table = jnp.concatenate(rows + [jnp.zeros((128 - FEATURES, q), F32)], axis=0)
        feat[k] = table.T[:, :FEATURES].astype(BF)

    ep[0:3, :] = -2.0 * p
    ep[3:4, :] = jnp.ones((1, q), F32)
    ep[4:5, :] = jnp.sum(p * p, axis=0, keepdims=True) + SOFTENING
    ep[5:8, :] = jnp.zeros((3, q), F32)
    lay(0)
    ep[0:3, :] = n
    ep[3:4, :] = jnp.zeros((1, q), F32)
    ep[4:5, :] = -jnp.sum(p * n, axis=0, keepdims=True)
    lay(1)
    pieces[...] = jnp.zeros_like(pieces)
    base[...] = jnp.zeros_like(base)
    row = lax.broadcasted_iota(jnp.int32, (devices, 1), 0)
    row_owner = (row % nbx) * nby + row // nbx
    before = (
        lax.broadcasted_iota(jnp.int32, (sub, sub), 0) < lax.broadcasted_iota(jnp.int32, (sub, sub), 1)
    ).astype(F32).astype(BF)
    ranks = lax.broadcasted_iota(jnp.int32, (128, 1), 0).astype(F32)
    times = lax.broadcasted_iota(jnp.int32, (samples, 1), 0)

    def one_tile(t, carry):
        o0 = pl.multiple_of(t * tile, tile)
        here = pl.ds(o0, tile)
        e = split3(eo[:, here])
        of = jnp.concatenate(
            [e[0]] * 3 + [e[1]] * 3 + [e[2]] * 3 + [jnp.zeros_like(e[0])], axis=0
        ).astype(BF)

        def one_chunk(c, acc):
            q0 = pl.multiple_of(c * chunk, chunk)
            rows = pl.ds(q0, chunk)
            inverse = lax.rsqrt(dot(feat[0, rows, :], of))
            near = dot(feat[1, rows, :], of) * inverse * inverse
            far = near * inverse
            acc = acc + dot(src[0, :, rows], inverse.astype(BF))
            acc = acc + dot(src[1, :, rows], near.astype(BF))
            return acc + dot(src[2, :, rows], far.astype(BF))

        history = lax.fori_loop(0, q // chunk, one_chunk, jnp.zeros((samples, tile), F32))
        slot = slots[:, here]
        frac = fracs[:, here]
        weights = jnp.where(times == slot, 1.0 - frac, 0.0) + jnp.where(times == slot + 1, frac, 0.0)
        value = jnp.sum(history * weights, axis=0, keepdims=True)
        parts = split3(value)
        owner = owners[:, here]
        mine = owner == row_owner
        hot = jnp.where(mine, 1.0, 0.0)
        seen = base[...]
        ranks_here = []
        for s in range(tile // sub):
            part = hot[:, s * sub:(s + 1) * sub]
            earlier = dot(part.astype(BF), before) + seen[:, 0:1]
            ranks_here.append(jnp.sum(part * earlier, axis=0, keepdims=True))
            seen = seen + jnp.sum(part, axis=1, keepdims=True)
        base[...] = seen
        rank = jnp.concatenate(ranks_here, axis=1)
        at_rank = jnp.where(rank == ranks, 1.0, 0.0).astype(BF)
        loads = jnp.concatenate([jnp.where(mine, v, 0.0) for v in parts], axis=0).astype(BF)
        pieces[...] += dot_nt(loads, at_rank)
        return carry

    lax.fori_loop(0, m // tile, one_tile, 0)
    packet[...] = pieces[0:devices, :] + pieces[devices:2 * devices, :] + pieces[2 * devices:, :]


def box_kernel(nbx, nby, obs_in, slots_in, fracs_in, owners_in, pts_in, nrm_in, src_in, cells_in, ground_in, fields,
               pz, us, vs, ws, pa, pb, flags, zmat, hot_own, hot_lr, hot_du, bt,
               gathered, agg, arrived, passed, passed_cells, obs, slots, fracs, owners, pts, nrm, src, cells, ground,
               packet, eo, ep, feat, pieces, base, in_sem, load_sem, raw_send, raw_recv, one_send, one_recv,
               two_send, two_recv, nb_send, nb_recv, rim_send, rim_recv):
    bx = lax.axis_index("bx")
    by = lax.axis_index("by")
    gx, gy, gz = fields.shape[1:]
    arrivals = nbx * 128
    has = (bx > 0, bx < nbx - 1, by > 0, by < nby - 1)
    to = (
        (jnp.maximum(bx - 1, 0), by),
        (jnp.minimum(bx + 1, nbx - 1), by),
        (bx, jnp.maximum(by - 1, 0)),
        (bx, jnp.minimum(by + 1, nby - 1)),
    )
    back = (1, 0, 3, 2)

    fetched = [
        pltpu.make_async_copy(a, b, in_sem.at[i])
        for i, (a, b) in enumerate((
            (cells_in.at[0], cells), (ground_in, ground), (src_in, src), (obs_in, obs), (slots_in, slots),
            (fracs_in, fracs), (owners_in, owners), (pts_in, pts), (nrm_in, nrm),
        ))
    ]
    for copy in fetched:
        copy.start()
    barrier = pltpu.get_barrier_semaphore()
    for i in range(1, nby):
        pl.semaphore_signal(barrier, inc=1, device_id=(bx, lax.rem(by + i, nby)), device_id_type=MESH)
    for i in range(1, nbx):
        pl.semaphore_signal(barrier, inc=1, device_id=(lax.rem(bx + i, nbx), by), device_id_type=MESH)
    pl.semaphore_wait(barrier, nby - 1 + nbx - 1)

    def remote(src, dst, send, recv, target):
        return pltpu.make_async_remote_copy(
            src_ref=src, dst_ref=dst, send_sem=send, recv_sem=recv, device_id=target, device_id_type=MESH
        )

    x_core = pl.ds(WIDE, gx)
    y_core = pl.ds(PAD, gy)
    give_p = (
        fields.at[0, pl.ds(0, WIDE)],
        fields.at[0, pl.ds(gx - WIDE, WIDE)],
        fields.at[0, :, pl.ds(0, PAD)],
        fields.at[0, :, pl.ds(gy - PAD, PAD)],
    )
    give_v = (
        fields.at[1, pl.ds(0, REACH)],
        fields.at[1, pl.ds(gx - REACH, REACH)],
        fields.at[2, :, pl.ds(0, PAD)],
        fields.at[2, :, pl.ds(gy - PAD, PAD)],
    )

    def rim(ref):
        return (
            ref.at[pl.ds(0, WIDE), y_core],
            ref.at[pl.ds(WIDE + gx, WIDE), y_core],
            ref.at[x_core, pl.ds(0, PAD)],
            ref.at[x_core, pl.ds(PAD + gy, PAD)],
        )

    rim_a = rim(pa)
    rim_b = rim(pb)
    rim_v = (
        us.at[pl.ds(0, REACH)],
        us.at[pl.ds(REACH + gx, REACH)],
        vs.at[:, pl.ds(0, PAD)],
        vs.at[:, pl.ds(PAD + gy, PAD)],
    )

    raw = []
    for s in range(4):
        raw.append((
            remote(cells_in.at[0], passed_cells.at[back[s]], raw_send.at[s], raw_recv.at[s], to[s]),
            remote(give_p[s], rim_a[back[s]], raw_send.at[4 + s], raw_recv.at[4 + s], to[s]),
            remote(give_v[s], rim_v[back[s]], raw_send.at[8 + s], raw_recv.at[8 + s], to[s]),
        ))

    def landed(src, dst, recv, s):
        return remote(src, dst, raw_send.at[s], recv, to[s % 4])

    for s in range(4):
        @pl.when(has[s])
        def _(s=s):
            for copy in raw[s]:
                copy.start()

    loads = [
        pltpu.make_async_copy(fields.at[0], pa.at[x_core, y_core], load_sem.at[0]),
        pltpu.make_async_copy(fields.at[1], us.at[pl.ds(REACH, gx)], load_sem.at[1]),
        pltpu.make_async_copy(fields.at[2], vs.at[:, y_core], load_sem.at[2]),
        pltpu.make_async_copy(fields.at[3], ws, load_sem.at[3]),
    ]
    for copy in loads:
        copy.start()

    for s in range(4):
        @pl.when(jnp.logical_not(has[s]))
        def _(s=s):
            rim_a[s][...] = jnp.zeros(rim_a[s].shape, F32)
            rim_b[s][...] = jnp.zeros(rim_b[s].shape, F32)
            rim_v[s][...] = jnp.zeros(rim_v[s].shape, F32)

    scaled = [DT * w for w in WEIGHTS]
    source = lax.broadcasted_iota(jnp.int32, (gz, 2 * gz), 0)
    column = lax.broadcasted_iota(jnp.int32, (gz, 2 * gz), 1)
    difference = jnp.zeros((gz, 2 * gz), F32)
    for j, w in enumerate(scaled, 1):
        difference = jnp.where(jnp.logical_and(column < gz, source - column == j), w, difference)
        difference = jnp.where(jnp.logical_and(column < gz, column - source == j), -w, difference)
        difference = jnp.where(jnp.logical_and(column >= gz, source + column - gz + 1 == j), -w, difference)
    coarse = difference.astype(BF)
    zmat[0:gz, :] = coarse
    zmat[gz:2 * gz, :] = coarse
    zmat[2 * gz:, :] = (difference - coarse.astype(F32)).astype(BF)

    for copy in fetched:
        copy.wait()
    ground_t = ground[...].astype(F32).T
    for x in range(gx):
        flags[x] = jnp.broadcast_to(ground_t[:, x:x + 1], (gy, gz))

    panel_part(nbx, nby, obs, slots, fracs, owners, pts, nrm, src, packet, eo, ep, feat, pieces, base)
    firsts = []
    for i in range(1, nby):
        peer = lax.rem(by + i, nby)
        rows = pl.ds(pl.multiple_of(peer * nbx, nbx), nbx)
        copy = remote(packet.at[rows, :], gathered.at[i], one_send.at[i], one_recv.at[i], (bx, peer))
        copy.start()
        firsts.append(copy)

    def fill(ref, rows, row_id):
        step = min(256, rows)

        def go(i, carry):
            r0 = pl.multiple_of(i * step, step)
            ids = lax.broadcasted_iota(jnp.int32, (step, 1), 0) + r0
            for b in range(nbx):
                ref[pl.ds(r0, step), b * 128:(b + 1) * 128] = jnp.where(
                    ids == row_id[b:b + 1, :], 1.0, 0.0
                ).astype(BF)
            return carry

        lax.fori_loop(0, rows // step, go, 0)

    fill(hot_own, gx * gy, cells[...] // gz)

    for copy in firsts:
        copy.wait_recv()
    mine = pl.ds(pl.multiple_of(by * nbx, nbx), nbx)
    total = packet[mine, :]
    for i in range(1, nby):
        total = total + gathered[i]
    for i in range(nbx):
        agg[i] = total[i:i + 1, :]
    seconds = []
    for i in range(1, nbx):
        peer = lax.rem(bx + i, nbx)
        copy = remote(agg.at[peer], arrived.at[bx], two_send.at[i], two_recv.at[i], (peer, by))
        copy.start()
        seconds.append(copy)
    arrived[bx] = agg[bx]

    for s in range(4):
        @pl.when(has[s])
        def _(s=s):
            landed(cells_in.at[0], passed_cells.at[s], raw_recv.at[back[s]], s).wait_recv()
            row_id = passed_cells[s] // gz
            if s == 0:
                fill(hot_lr.at[0], WIDE * gy, row_id - (gx - WIDE) * gy)
            elif s == 1:
                fill(hot_lr.at[1], WIDE * gy, row_id)
            else:
                y = row_id % gy - (gy - PAD if s == 2 else 0)
                inside = jnp.logical_and(y >= 0, y < PAD)
                fill(hot_du.at[s - 2], gx * PAD, jnp.where(inside, row_id // gy * PAD + y, -1))

    heights = lax.broadcasted_iota(jnp.int32, (gz, 1), 0)

    def targets(values, cell_rows):
        for b in range(nbx):
            v = values(b)
            at = heights == cell_rows[b:b + 1, :] % gz
            hi = v.astype(BF).astype(F32)
            bt[0:gz, b * 128:(b + 1) * 128] = jnp.where(at, hi, 0.0).astype(BF)
            bt[gz:2 * gz, b * 128:(b + 1) * 128] = jnp.where(at, v - hi, 0.0).astype(BF)

    def added(hot):
        both = dot_nt(hot, bt[...])
        return both[:, :gz] + both[:, gz:]

    for copy in seconds:
        copy.wait_recv()
    handed = [
        remote(arrived, passed.at[back[s]], nb_send.at[s], nb_recv.at[s], to[s]) for s in range(4)
    ]
    for s in range(4):
        @pl.when(has[s])
        def _(s=s):
            handed[s].start()

    targets(lambda b: arrived[b], cells[...])
    loads[0].wait()
    planes = min(4, gx)
    ends = 2

    def inject_own(i, carry):
        r0 = pl.multiple_of(i * planes * gy, planes * gy)
        extra = added(hot_own[pl.ds(r0, planes * gy), :]).reshape(planes, gy, gz)
        pa[pl.ds(WIDE + i * planes, planes), PAD:PAD + gy, :] += extra
        return carry

    lax.fori_loop(0, gx // planes, inject_own, 0)

    for s in range(4):
        @pl.when(has[s])
        def _(s=s):
            landed(give_p[s], rim_a[s], raw_recv.at[4 + back[s]], 4 + s).wait_recv()
            landed(give_v[s], rim_v[s], raw_recv.at[8 + back[s]], 8 + s).wait_recv()
            remote(arrived, passed.at[s], nb_send.at[s], nb_recv.at[back[s]], to[s]).wait_recv()
            targets(lambda b: passed[s, b], passed_cells[s])
            if s < 2:
                x0 = 0 if s == 0 else WIDE + gx

                def inject_x(i, carry):
                    r0 = pl.multiple_of(i * gy, gy)
                    pa[x0 + i, PAD:PAD + gy, :] += added(hot_lr[s, pl.ds(r0, gy), :])
                    return carry

                lax.fori_loop(0, WIDE, inject_x, 0)
            else:
                y0 = 0 if s == 2 else PAD + gy
                pa[WIDE:WIDE + gx, y0:y0 + PAD, :] += added(hot_du[s - 2]).reshape(gx, PAD, gz)

    for copy in loads[1:]:
        copy.wait()

    def z_term(f, flag):
        high = f.astype(BF)
        low = (f - high.astype(F32)).astype(BF)
        both = dot(jnp.concatenate([high, low, high], axis=1), zmat[...])
        return both[:, :gz] + flag * both[:, gz:]

    def span(get):
        total = None
        for j, w in enumerate(scaled, 1):
            term = w * (get(j) - get(-j))
            total = term if total is None else total + term
        return total

    def loop(lo, hi, step):
        def go(i, carry):
            step(i)
            return carry

        lax.fori_loop(lo, hi, go, 0)

    def u_plane(p, i):
        us[i] = us[i] - span(lambda j: p[i + REACH + j, PAD:PAD + gy, :])

    def v_rows(p, x, lo, hi):
        vs[x, lo:hi, :] = vs[x, lo:hi, :] - span(lambda j: p[x + WIDE, lo + j:hi + j, :])

    def w_planes(p, new, x, shift):
        rows = planes * gy
        shift_y = PAD if shift else 0
        f = p[pl.ds(x + WIDE, planes), PAD:PAD + gy, :].reshape(rows, gz)
        flag = flags[pl.ds(x, planes)].reshape(rows, gz)
        w = ws[pl.ds(x, planes)].reshape(rows, gz) - z_term(f, flag)
        ws[pl.ds(x, planes)] = w.reshape(planes, gy, gz)
        new[pl.ds(x + shift, planes), shift_y:shift_y + gy, :] = (f - z_term(w, -flag)).reshape(planes, gy, gz)

    def p_rows(p, x, lo, hi):
        change = span(lambda j: us[x + REACH + j, lo:hi, :])
        change = change + span(lambda j: vs[x, PAD + lo + j:PAD + hi + j, :])
        p[x + WIDE, PAD + lo:PAD + hi, :] = p[x + WIDE, PAD + lo:PAD + hi, :] - change

    def outer_u(p, s):
        lo = 0 if s == 0 else REACH + gx

        @pl.when(has[s])
        def _():
            loop(lo, lo + REACH, lambda i: u_plane(p, i))

    def outer_v(p, s):
        lo = PAD - REACH if s == 2 else PAD + gy

        @pl.when(has[s])
        def _():
            loop(0, gx, lambda x: v_rows(p, x, lo, lo + REACH))

    for s in (0, 1):
        outer_u(pa, s)
    for s in (2, 3):
        outer_v(pa, s)

    def first_velocity(x):
        u_plane(pa, x + REACH)
        v_rows(pa, x, PAD, PAD + gy)

    loop(0, gx, first_velocity)
    third = gx // planes - 2 * ends

    def w_blocks(p, new, lo, hi, shift):
        loop(lo, hi, lambda i: w_planes(p, new, i * planes, shift))

    w_blocks(pa, pb, 0, ends, WIDE)
    w_blocks(pa, pb, ends + third, 2 * ends + third, WIDE)

    give_b = (
        pb.at[pl.ds(WIDE, WIDE), y_core],
        pb.at[pl.ds(gx, WIDE), y_core],
        pb.at[x_core, pl.ds(PAD, PAD)],
        pb.at[x_core, pl.ds(gy, PAD)],
    )
    second_rim = [
        remote(give_b[s], rim_b[back[s]], rim_send.at[s], rim_recv.at[s], to[s]) for s in range(4)
    ]

    def send_rim(s):
        @pl.when(has[s])
        def _():
            second_rim[s].start()

    loop(0, WIDE, lambda x: p_rows(pb, x, 0, gy))
    send_rim(0)
    loop(gx - WIDE, gx, lambda x: p_rows(pb, x, 0, gy))
    send_rim(1)
    w_blocks(pa, pb, ends, ends + third, WIDE)

    def edges(x):
        p_rows(pb, x, 0, PAD)
        p_rows(pb, x, gy - PAD, gy)

    loop(WIDE, gx - WIDE, edges)
    send_rim(2)
    send_rim(3)
    loop(WIDE, gx - WIDE, lambda x: p_rows(pb, x, PAD, gy - PAD))

    w_blocks(pb, pz, 0, gx // planes, 0)
    loop(0, gx, lambda x: v_rows(pb, x, 2 * PAD, gy))
    loop(2 * REACH, gx, lambda i: u_plane(pb, i))
    for s in range(4):
        @pl.when(has[s])
        def _(s=s):
            remote(give_b[s], rim_b[s], rim_send.at[s], rim_recv.at[back[s]], to[s]).wait_recv()
    for s in (0, 1):
        outer_u(pb, s)
    loop(REACH, 2 * REACH, lambda i: u_plane(pb, i))
    loop(gx, gx + REACH, lambda i: u_plane(pb, i))
    for s in (2, 3):
        outer_v(pb, s)

    def outer_rows(x):
        v_rows(pb, x, PAD, 2 * PAD)
        v_rows(pb, x, gy, gy + PAD)

    loop(0, gx, outer_rows)

    for copy in firsts + seconds:
        copy.wait_send()
    for s in range(4):
        @pl.when(has[s])
        def _(s=s):
            for copy in raw[s]:
                copy.wait_send()
            handed[s].wait_send()
            second_rim[s].wait_send()


def last_kernel(pz, us, vs, ws, out, held, sems):
    gx, gy, gz = ws.shape
    step = min(8, gx)
    copies = [
        pltpu.make_async_copy(us.at[pl.ds(REACH, gx)], out.at[1], sems.at[0]),
        pltpu.make_async_copy(vs.at[:, pl.ds(PAD, gy)], out.at[2], sems.at[1]),
        pltpu.make_async_copy(ws, out.at[3], sems.at[2]),
    ]
    for copy in copies:
        copy.start()
    for part in range(gx // step):
        def plane(i, carry):
            x = part * step + i
            change = None
            for j, w in enumerate(WEIGHTS, 1):
                term = (DT * w) * (
                    us[x + REACH + j] - us[x + REACH - j]
                    + (vs[x, PAD + j:PAD + gy + j, :] - vs[x, PAD - j:PAD + gy - j, :])
                )
                change = term if change is None else change + term
            held[x] = pz[x] - change
            return carry

        lax.fori_loop(0, step, plane, 0)
        rows = pl.ds(part * step, step)
        copy = pltpu.make_async_copy(held.at[rows], out.at[0, rows], sems.at[3 + part])
        copy.start()
        copies.append(copy)
    for copy in copies:
        copy.wait()


def vmem():
    return pl.BlockSpec(memory_space=pltpu.VMEM)


def anywhere():
    return pl.BlockSpec(memory_space=pl.ANY)


def body(nbx, nby, fields, ground, observers, slots, fractions, owners, arrival_cell, panel_points, panel_normals,
         sources):
    devices = nbx * nby
    m = observers.shape[1]
    q = panel_points.shape[1]
    gx, gy, gz = fields.shape[1:]
    k = nbx * 128
    dma = pltpu.SemaphoreType.DMA
    wide = (gx + 2 * WIDE, gy + 2 * PAD, gz)
    kept = ((gx, gy, gz), (gx + 2 * REACH, gy, gz), (gx, gy + 2 * PAD, gz), (gx, gy, gz))
    sems = (9, 4, 12, 12, nby, nby, nbx, nbx, 4, 4, 4, 4)
    state = pl.pallas_call(
        functools.partial(box_kernel, nbx, nby),
        out_shape=[jax.ShapeDtypeStruct(shape, F32) for shape in kept],
        in_specs=[pl.BlockSpec(memory_space=pltpu.HBM)] * 10,
        out_specs=[vmem()] * 4,
        scratch_shapes=[
            pltpu.VMEM(wide, F32),
            pltpu.VMEM(wide, F32),
            pltpu.VMEM((gx, gy, gz), F32),
            pltpu.VMEM((3 * gz, 2 * gz), BF),
            pltpu.VMEM((gx * gy, k), BF),
            pltpu.VMEM((2, WIDE * gy, k), BF),
            pltpu.VMEM((2, gx * PAD, k), BF),
            pltpu.VMEM((2 * gz, k), BF),
            pltpu.VMEM((nby, nbx, 128), F32),
            pltpu.VMEM((nbx, 1, 128), F32),
            pltpu.VMEM((nbx, 1, 128), F32),
            pltpu.VMEM((4, nbx, 1, 128), F32),
            pltpu.VMEM((4, nbx, 128), jnp.int32),
            pltpu.VMEM((3, m), F32),
            pltpu.VMEM((1, m), jnp.int32),
            pltpu.VMEM((1, m), F32),
            pltpu.VMEM((1, m), jnp.int32),
            pltpu.VMEM((3, q), F32),
            pltpu.VMEM((3, q), F32),
            pltpu.VMEM((3, sources.shape[2], q), BF),
            pltpu.VMEM((nbx, 128), jnp.int32),
            pltpu.VMEM((gx, gy), jnp.int32),
            pltpu.VMEM((devices, 128), F32),
        ] + panel_scratch(m, q, devices) + [dma((n,)) for n in sems],
        compiler_params=pltpu.CompilerParams(
            collective_id=0, has_side_effects=True, vmem_limit_bytes=42 << 20
        ),
        name="box",
    )(
        observers,
        slots.reshape(1, m),
        fractions.reshape(1, m),
        owners.reshape(1, m),
        panel_points,
        panel_normals,
        sources.transpose(0, 2, 1),
        arrival_cell,
        ground,
        fields,
    )
    return pl.pallas_call(
        last_kernel,
        out_shape=jax.ShapeDtypeStruct(fields.shape, F32),
        in_specs=[vmem()] * 4,
        out_specs=anywhere(),
        scratch_shapes=[pltpu.VMEM((gx, gy, gz), F32), dma((3 + gx // min(8, gx),))],
        compiler_params=pltpu.CompilerParams(vmem_limit_bytes=8 << 20),
        name="last",
    )(*state)


def solution(mesh):
    placed = (
        P(None, "bx", "by", None),
        P("bx", "by"),
        P(None, "bx"),
        P("bx"),
        P("bx"),
        P("bx", None),
        P(("bx", "by"), None, None),
        P(None, "by"),
        P(None, "by"),
        P(None, "by", None),
    )
    return jax.shard_map(
        functools.partial(body, mesh.shape["bx"], mesh.shape["by"]),
        mesh=mesh,
        in_specs=placed,
        out_specs=P(None, "bx", "by", None),
        check_vma=False,
    )
```

```python
import functools

import jax
import jax.numpy as jnp
from jax import lax
from jax.experimental import pallas as pl
from jax.experimental.pallas import tpu as pltpu
from jax.sharding import PartitionSpec as P

BF = jnp.bfloat16
F32 = jnp.float32
MESH = pl.DeviceIdType.MESH
WEIGHTS = (0.770882380518, -0.166705904415, 0.02084314277)
DT = 0.5
SOFTENING = 0.01
REACH = 3
WIDE = 6
PAD = 8
FEATURES = 80


def split3(x):
    a = x.astype(BF).astype(F32)
    r = x - a
    b = r.astype(BF).astype(F32)
    return a, b, r - b


def dot(a, b):
    return jnp.dot(a, b, preferred_element_type=F32)


def dot_nt(a, b):
    return lax.dot_general(a, b, (((1,), (1,)), ((), ())), preferred_element_type=F32)


def panel_scratch(m, q, devices):
    return [
        pltpu.VMEM((8, m), F32),
        pltpu.VMEM((8, q), F32),
        pltpu.VMEM((2, q, FEATURES), BF),
        pltpu.VMEM((3 * devices, 128), F32),
        pltpu.VMEM((devices, 128), F32),
    ]


def panel_part(nbx, nby, obs, slots, fracs, owners, pts, nrm, src, packet, eo, ep, feat, pieces, base):
    m = obs.shape[1]
    q = pts.shape[1]
    samples = src.shape[1]
    devices = nbx * nby
    tile = min(1024, m)
    chunk = min(512, q)
    sub = 256

    o = obs[...]
    eo[0:3, :] = o
    eo[3:4, :] = jnp.sum(o * o, axis=0, keepdims=True)
    eo[4:5, :] = jnp.ones((1, m), F32)
    eo[5:8, :] = jnp.zeros((3, m), F32)
    p = pts[...]
    n = nrm[...]

    def lay(k):
        s = split3(ep[...])
        rows = [s[0], s[1], s[2]] * 3 + [jnp.zeros_like(s[0])]
        table = jnp.concatenate(rows + [jnp.zeros((128 - FEATURES, q), F32)], axis=0)
        feat[k] = table.T[:, :FEATURES].astype(BF)

    ep[0:3, :] = -2.0 * p
    ep[3:4, :] = jnp.ones((1, q), F32)
    ep[4:5, :] = jnp.sum(p * p, axis=0, keepdims=True) + SOFTENING
    ep[5:8, :] = jnp.zeros((3, q), F32)
    lay(0)
    ep[0:3, :] = n
    ep[3:4, :] = jnp.zeros((1, q), F32)
    ep[4:5, :] = -jnp.sum(p * n, axis=0, keepdims=True)
    lay(1)
    pieces[...] = jnp.zeros_like(pieces)
    base[...] = jnp.zeros_like(base)
    row = lax.broadcasted_iota(jnp.int32, (devices, 1), 0)
    row_owner = (row % nbx) * nby + row // nbx
    before = (
        lax.broadcasted_iota(jnp.int32, (sub, sub), 0) < lax.broadcasted_iota(jnp.int32, (sub, sub), 1)
    ).astype(F32).astype(BF)
    ranks = lax.broadcasted_iota(jnp.int32, (128, 1), 0).astype(F32)
    times = lax.broadcasted_iota(jnp.int32, (samples, 1), 0)

    def one_tile(t, carry):
        o0 = pl.multiple_of(t * tile, tile)
        here = pl.ds(o0, tile)
        e = split3(eo[:, here])
        of = jnp.concatenate(
            [e[0]] * 3 + [e[1]] * 3 + [e[2]] * 3 + [jnp.zeros_like(e[0])], axis=0
        ).astype(BF)

        def one_chunk(c, acc):
            q0 = pl.multiple_of(c * chunk, chunk)
            rows = pl.ds(q0, chunk)
            inverse = lax.rsqrt(dot(feat[0, rows, :], of))
            near = dot(feat[1, rows, :], of) * inverse * inverse
            far = near * inverse
            acc = acc + dot(src[0, :, rows], inverse.astype(BF))
            acc = acc + dot(src[1, :, rows], near.astype(BF))
            return acc + dot(src[2, :, rows], far.astype(BF))

        history = lax.fori_loop(0, q // chunk, one_chunk, jnp.zeros((samples, tile), F32))
        slot = slots[:, here]
        frac = fracs[:, here]
        weights = jnp.where(times == slot, 1.0 - frac, 0.0) + jnp.where(times == slot + 1, frac, 0.0)
        value = jnp.sum(history * weights, axis=0, keepdims=True)
        parts = split3(value)
        owner = owners[:, here]
        mine = owner == row_owner
        hot = jnp.where(mine, 1.0, 0.0)
        seen = base[...]
        ranks_here = []
        for s in range(tile // sub):
            part = hot[:, s * sub:(s + 1) * sub]
            earlier = dot(part.astype(BF), before) + seen[:, 0:1]
            ranks_here.append(jnp.sum(part * earlier, axis=0, keepdims=True))
            seen = seen + jnp.sum(part, axis=1, keepdims=True)
        base[...] = seen
        rank = jnp.concatenate(ranks_here, axis=1)
        at_rank = jnp.where(rank == ranks, 1.0, 0.0).astype(BF)
        loads = jnp.concatenate([jnp.where(mine, v, 0.0) for v in parts], axis=0).astype(BF)
        pieces[...] += dot_nt(loads, at_rank)
        return carry

    lax.fori_loop(0, m // tile, one_tile, 0)
    packet[...] = pieces[0:devices, :] + pieces[devices:2 * devices, :] + pieces[2 * devices:, :]


def box_kernel(nbx, nby, obs_in, slots_in, fracs_in, owners_in, pts_in, nrm_in, src_in, cells_in, ground_in, fields,
               pz, us, vs, ws, pa, pb, flags, zmat, hot_own, hot_lr, hot_du, bt,
               gathered, agg, arrived, passed, passed_cells, obs, slots, fracs, owners, pts, nrm, src, cells, ground,
               packet, eo, ep, feat, pieces, base, in_sem, load_sem, raw_send, raw_recv, one_send, one_recv,
               two_send, two_recv, nb_send, nb_recv, rim_send, rim_recv):
    bx = lax.axis_index("bx")
    by = lax.axis_index("by")
    gx, gy, gz = fields.shape[1:]
    arrivals = nbx * 128
    has = (bx > 0, bx < nbx - 1, by > 0, by < nby - 1)
    to = (
        (jnp.maximum(bx - 1, 0), by),
        (jnp.minimum(bx + 1, nbx - 1), by),
        (bx, jnp.maximum(by - 1, 0)),
        (bx, jnp.minimum(by + 1, nby - 1)),
    )
    back = (1, 0, 3, 2)

    fetched = [
        pltpu.make_async_copy(a, b, in_sem.at[i])
        for i, (a, b) in enumerate((
            (cells_in.at[0], cells), (ground_in, ground), (src_in, src), (obs_in, obs), (slots_in, slots),
            (fracs_in, fracs), (owners_in, owners), (pts_in, pts), (nrm_in, nrm),
        ))
    ]
    for copy in fetched:
        copy.start()
    barrier = pltpu.get_barrier_semaphore()
    for i in range(1, nby):
        pl.semaphore_signal(barrier, inc=1, device_id=(bx, lax.rem(by + i, nby)), device_id_type=MESH)
    for i in range(1, nbx):
        pl.semaphore_signal(barrier, inc=1, device_id=(lax.rem(bx + i, nbx), by), device_id_type=MESH)

    def remote(src, dst, send, recv, target):
        return pltpu.make_async_remote_copy(
            src_ref=src, dst_ref=dst, send_sem=send, recv_sem=recv, device_id=target, device_id_type=MESH
        )

    x_core = pl.ds(WIDE, gx)
    y_core = pl.ds(PAD, gy)
    give_p = (
        fields.at[0, pl.ds(0, WIDE)],
        fields.at[0, pl.ds(gx - WIDE, WIDE)],
        fields.at[0, :, pl.ds(0, PAD)],
        fields.at[0, :, pl.ds(gy - PAD, PAD)],
    )
    give_v = (
        fields.at[1, pl.ds(0, REACH)],
        fields.at[1, pl.ds(gx - REACH, REACH)],
        fields.at[2, :, pl.ds(0, PAD)],
        fields.at[2, :, pl.ds(gy - PAD, PAD)],
    )

    def rim(ref):
        return (
            ref.at[pl.ds(0, WIDE), y_core],
            ref.at[pl.ds(WIDE + gx, WIDE), y_core],
            ref.at[x_core, pl.ds(0, PAD)],
            ref.at[x_core, pl.ds(PAD + gy, PAD)],
        )

    rim_a = rim(pa)
    rim_b = rim(pb)
    rim_v = (
        us.at[pl.ds(0, REACH)],
        us.at[pl.ds(REACH + gx, REACH)],
        vs.at[:, pl.ds(0, PAD)],
        vs.at[:, pl.ds(PAD + gy, PAD)],
    )

    raw = []
    for s in range(4):
        raw.append((
            remote(cells_in.at[0], passed_cells.at[back[s]], raw_send.at[s], raw_recv.at[s], to[s]),
            remote(give_p[s], rim_a[back[s]], raw_send.at[4 + s], raw_recv.at[4 + s], to[s]),
            remote(give_v[s], rim_v[back[s]], raw_send.at[8 + s], raw_recv.at[8 + s], to[s]),
        ))

    def landed(src, dst, recv, s):
        return remote(src, dst, raw_send.at[s], recv, to[s % 4])

    loads = [
        pltpu.make_async_copy(fields.at[0], pa.at[x_core, y_core], load_sem.at[0]),
        pltpu.make_async_copy(fields.at[1], us.at[pl.ds(REACH, gx)], load_sem.at[1]),
        pltpu.make_async_copy(fields.at[2], vs.at[:, y_core], load_sem.at[2]),
        pltpu.make_async_copy(fields.at[3], ws, load_sem.at[3]),
    ]
    for copy in loads:
        copy.start()

    for s in range(4):
        @pl.when(jnp.logical_not(has[s]))
        def _(s=s):
            rim_a[s][...] = jnp.zeros(rim_a[s].shape, F32)
            rim_b[s][...] = jnp.zeros(rim_b[s].shape, F32)
            rim_v[s][...] = jnp.zeros(rim_v[s].shape, F32)

    scaled = [DT * w for w in WEIGHTS]
    source = lax.broadcasted_iota(jnp.int32, (gz, 2 * gz), 0)
    column = lax.broadcasted_iota(jnp.int32, (gz, 2 * gz), 1)
    difference = jnp.zeros((gz, 2 * gz), F32)
    for j, w in enumerate(scaled, 1):
        difference = jnp.where(jnp.logical_and(column < gz, source - column == j), w, difference)
        difference = jnp.where(jnp.logical_and(column < gz, column - source == j), -w, difference)
        difference = jnp.where(jnp.logical_and(column >= gz, source + column - gz + 1 == j), -w, difference)
    coarse = difference.astype(BF)
    zmat[0:gz, :] = coarse
    zmat[gz:2 * gz, :] = coarse
    zmat[2 * gz:, :] = (difference - coarse.astype(F32)).astype(BF)

    for copy in fetched:
        copy.wait()
    ground_t = ground[...].astype(F32).T
    for x in range(gx):
        flags[x] = jnp.broadcast_to(ground_t[:, x:x + 1], (gy, gz))

    pl.semaphore_wait(barrier, nby - 1 + nbx - 1)
    for s in range(4):
        @pl.when(has[s])
        def _(s=s):
            for copy in raw[s]:
                copy.start()

    panel_part(nbx, nby, obs, slots, fracs, owners, pts, nrm, src, packet, eo, ep, feat, pieces, base)
    firsts = []
    for i in range(1, nby):
        peer = lax.rem(by + i, nby)
        rows = pl.ds(pl.multiple_of(peer * nbx, nbx), nbx)
        copy = remote(packet.at[rows, :], gathered.at[i], one_send.at[i], one_recv.at[i], (bx, peer))
        copy.start()
        firsts.append(copy)

    def fill(ref, rows, row_id):
        step = min(256, rows)

        def go(i, carry):
            r0 = pl.multiple_of(i * step, step)
            ids = lax.broadcasted_iota(jnp.int32, (step, 1), 0) + r0
            for b in range(nbx):
                ref[pl.ds(r0, step), b * 128:(b + 1) * 128] = jnp.where(
                    ids == row_id[b:b + 1, :], 1.0, 0.0
                ).astype(BF)
            return carry

        lax.fori_loop(0, rows // step, go, 0)

    fill(hot_own, gx * gy, cells[...] // gz)

    for copy in firsts:
        copy.wait_recv()
    mine = pl.ds(pl.multiple_of(by * nbx, nbx), nbx)
    total = packet[mine, :]
    for i in range(1, nby):
        total = total + gathered[i]
    for i in range(nbx):
        agg[i] = total[i:i + 1, :]
    seconds = []
    for i in range(1, nbx):
        peer = lax.rem(bx + i, nbx)
        copy = remote(agg.at[peer], arrived.at[bx], two_send.at[i], two_recv.at[i], (peer, by))
        copy.start()
        seconds.append(copy)
    arrived[bx] = agg[bx]

    for s in range(4):
        @pl.when(has[s])
        def _(s=s):
            landed(cells_in.at[0], passed_cells.at[s], raw_recv.at[back[s]], s).wait_recv()
            row_id = passed_cells[s] // gz
            if s == 0:
                fill(hot_lr.at[0], WIDE * gy, row_id - (gx - WIDE) * gy)
            elif s == 1:
                fill(hot_lr.at[1], WIDE * gy, row_id)
            else:
                y = row_id % gy - (gy - PAD if s == 2 else 0)
                inside = jnp.logical_and(y >= 0, y < PAD)
                fill(hot_du.at[s - 2], gx * PAD, jnp.where(inside, row_id // gy * PAD + y, -1))

    heights = lax.broadcasted_iota(jnp.int32, (gz, 1), 0)

    def targets(bt, values, cell_rows):
        for b in range(nbx):
            v = values(b)
            at = heights == cell_rows[b:b + 1, :] % gz
            hi = v.astype(BF).astype(F32)
            bt[0:gz, b * 128:(b + 1) * 128] = jnp.where(at, hi, 0.0).astype(BF)
            bt[gz:2 * gz, b * 128:(b + 1) * 128] = jnp.where(at, v - hi, 0.0).astype(BF)

    def added(hot, bt):
        both = dot_nt(hot, bt[...])
        return both[:, :gz] + both[:, gz:]

    for copy in seconds:
        copy.wait_recv()
    handed = [
        remote(arrived, passed.at[back[s]], nb_send.at[s], nb_recv.at[s], to[s]) for s in range(4)
    ]
    for s in range(4):
        @pl.when(has[s])
        def _(s=s):
            handed[s].start()

    own, theirs = bt.at[0], bt.at[1]
    targets(own, lambda b: arrived[b], cells[...])
    loads[0].wait()
    planes = min(4, gx)
    ends = 2
    near = min(2 * WIDE, gx // 2)

    def inject_own(lo, hi):
        count = hi - lo
        step = next(n for n in (6, 4, 2, 1) if count % n == 0)

        def go(i, carry):
            x = lo + i * step
            rows = pl.ds(pl.multiple_of(x * gy, gy), step * gy)
            pa[pl.ds(WIDE + x, step), PAD:PAD + gy, :] += added(hot_own[rows, :], own).reshape(step, gy, gz)
            return carry

        lax.fori_loop(0, count // step, go, 0)

    inject_own(0, near)
    inject_own(gx - near, gx)

    for s in range(4):
        @pl.when(has[s])
        def _(s=s):
            landed(give_p[s], rim_a[s], raw_recv.at[4 + back[s]], 4 + s).wait_recv()
            landed(give_v[s], rim_v[s], raw_recv.at[8 + back[s]], 8 + s).wait_recv()
            remote(arrived, passed.at[s], nb_send.at[s], nb_recv.at[back[s]], to[s]).wait_recv()
            targets(theirs, lambda b: passed[s, b], passed_cells[s])
            if s < 2:
                x0 = 0 if s == 0 else WIDE + gx
                pa[x0:x0 + WIDE, PAD:PAD + gy, :] += added(hot_lr[s], theirs).reshape(WIDE, gy, gz)
            else:
                y0 = 0 if s == 2 else PAD + gy
                pa[WIDE:WIDE + gx, y0:y0 + PAD, :] += added(hot_du[s - 2], theirs).reshape(gx, PAD, gz)

    for copy in loads[1:]:
        copy.wait()

    def z_term(f, flag):
        high = f.astype(BF)
        low = (f - high.astype(F32)).astype(BF)
        both = dot(jnp.concatenate([high, low, high], axis=1), zmat[...])
        return both[:, :gz] + flag * both[:, gz:]

    def span(get):
        total = None
        for j, w in enumerate(scaled, 1):
            term = w * (get(j) - get(-j))
            total = term if total is None else total + term
        return total

    def loop(lo, hi, step):
        def go(i, carry):
            step(i)
            return carry

        lax.fori_loop(lo, hi, go, 0)

    def u_plane(p, i):
        us[i] = us[i] - span(lambda j: p[i + REACH + j, PAD:PAD + gy, :])

    def v_rows(p, x, lo, hi):
        vs[x, lo:hi, :] = vs[x, lo:hi, :] - span(lambda j: p[x + WIDE, lo + j:hi + j, :])

    def w_planes(p, new, x, shift):
        rows = planes * gy
        shift_y = PAD if shift else 0
        f = p[pl.ds(x + WIDE, planes), PAD:PAD + gy, :].reshape(rows, gz)
        flag = flags[pl.ds(x, planes)].reshape(rows, gz)
        w = ws[pl.ds(x, planes)].reshape(rows, gz) - z_term(f, flag)
        ws[pl.ds(x, planes)] = w.reshape(planes, gy, gz)
        new[pl.ds(x + shift, planes), shift_y:shift_y + gy, :] = (f - z_term(w, -flag)).reshape(planes, gy, gz)

    def p_rows(p, x, lo, hi):
        change = span(lambda j: us[x + REACH + j, lo:hi, :])
        change = change + span(lambda j: vs[x, PAD + lo + j:PAD + hi + j, :])
        p[x + WIDE, PAD + lo:PAD + hi, :] = p[x + WIDE, PAD + lo:PAD + hi, :] - change

    def outer_u(p, s):
        lo = 0 if s == 0 else REACH + gx

        @pl.when(has[s])
        def _():
            loop(lo, lo + REACH, lambda i: u_plane(p, i))

    def outer_v(p, s, x0, x1):
        lo = PAD - REACH if s == 2 else PAD + gy

        @pl.when(has[s])
        def _():
            loop(x0, x1, lambda x: v_rows(p, x, lo, lo + REACH))

    for s in (0, 1):
        outer_u(pa, s)
    for s in (2, 3):
        outer_v(pa, s, 0, WIDE)
        outer_v(pa, s, gx - WIDE, gx)

    few = min(WIDE + REACH, gx // 2)
    loop(REACH, REACH + few, lambda i: u_plane(pa, i))
    loop(REACH + gx - few, REACH + gx, lambda i: u_plane(pa, i))
    loop(0, WIDE, lambda x: v_rows(pa, x, PAD, PAD + gy))
    loop(gx - WIDE, gx, lambda x: v_rows(pa, x, PAD, PAD + gy))
    third = gx // planes - 2 * ends

    def w_blocks(p, new, lo, hi, shift):
        loop(lo, hi, lambda i: w_planes(p, new, i * planes, shift))

    w_blocks(pa, pb, 0, ends, WIDE)
    w_blocks(pa, pb, ends + third, 2 * ends + third, WIDE)

    give_b = (
        pb.at[pl.ds(WIDE, WIDE), y_core],
        pb.at[pl.ds(gx, WIDE), y_core],
        pb.at[x_core, pl.ds(PAD, PAD)],
        pb.at[x_core, pl.ds(gy, PAD)],
    )
    second_rim = [
        remote(give_b[s], rim_b[back[s]], rim_send.at[s], rim_recv.at[s], to[s]) for s in range(4)
    ]

    def send_rim(s):
        @pl.when(has[s])
        def _():
            second_rim[s].start()

    loop(0, WIDE, lambda x: p_rows(pb, x, 0, gy))
    send_rim(0)
    loop(gx - WIDE, gx, lambda x: p_rows(pb, x, 0, gy))
    send_rim(1)
    if gx > 2 * near:
        inject_own(near, gx - near)
    for s in (2, 3):
        outer_v(pa, s, WIDE, gx - WIDE)
    loop(WIDE, gx - WIDE, lambda x: v_rows(pa, x, PAD, PAD + gy))
    w_blocks(pa, pb, ends, ends + third, WIDE)
    loop(REACH + few, REACH + gx - few, lambda i: u_plane(pa, i))

    def edges(x):
        p_rows(pb, x, 0, PAD)
        p_rows(pb, x, gy - PAD, gy)

    loop(WIDE, gx - WIDE, edges)
    send_rim(2)
    send_rim(3)
    loop(WIDE, gx - WIDE, lambda x: p_rows(pb, x, PAD, gy - PAD))

    w_blocks(pb, pz, 0, gx // planes, 0)
    loop(0, gx, lambda x: v_rows(pb, x, 2 * PAD, gy))
    loop(2 * REACH, gx, lambda i: u_plane(pb, i))
    for s in range(4):
        @pl.when(has[s])
        def _(s=s):
            remote(give_b[s], rim_b[s], rim_send.at[s], rim_recv.at[back[s]], to[s]).wait_recv()
    for s in (0, 1):
        outer_u(pb, s)
    loop(REACH, 2 * REACH, lambda i: u_plane(pb, i))
    loop(gx, gx + REACH, lambda i: u_plane(pb, i))
    for s in (2, 3):
        outer_v(pb, s, 0, gx)

    def outer_rows(x):
        v_rows(pb, x, PAD, 2 * PAD)
        v_rows(pb, x, gy, gy + PAD)

    loop(0, gx, outer_rows)

    for copy in firsts + seconds:
        copy.wait_send()
    for s in range(4):
        @pl.when(has[s])
        def _(s=s):
            for copy in raw[s]:
                copy.wait_send()
            handed[s].wait_send()
            second_rim[s].wait_send()


def last_kernel(pz, us, vs, ws, out, held, sems):
    gx, gy, gz = ws.shape
    step = min(8, gx)
    copies = [
        pltpu.make_async_copy(us.at[pl.ds(REACH, gx)], out.at[1], sems.at[0]),
        pltpu.make_async_copy(vs.at[:, pl.ds(PAD, gy)], out.at[2], sems.at[1]),
        pltpu.make_async_copy(ws, out.at[3], sems.at[2]),
    ]
    for copy in copies:
        copy.start()
    for part in range(gx // step):
        def plane(i, carry):
            x = part * step + i
            change = None
            for j, w in enumerate(WEIGHTS, 1):
                term = (DT * w) * (
                    us[x + REACH + j] - us[x + REACH - j]
                    + (vs[x, PAD + j:PAD + gy + j, :] - vs[x, PAD - j:PAD + gy - j, :])
                )
                change = term if change is None else change + term
            held[x] = pz[x] - change
            return carry

        lax.fori_loop(0, step, plane, 0)
        rows = pl.ds(part * step, step)
        copy = pltpu.make_async_copy(held.at[rows], out.at[0, rows], sems.at[3 + part])
        copy.start()
        copies.append(copy)
    for copy in copies:
        copy.wait()


def vmem():
    return pl.BlockSpec(memory_space=pltpu.VMEM)


def anywhere():
    return pl.BlockSpec(memory_space=pl.ANY)


def body(nbx, nby, fields, ground, observers, slots, fractions, owners, arrival_cell, panel_points, panel_normals,
         sources):
    devices = nbx * nby
    m = observers.shape[1]
    q = panel_points.shape[1]
    gx, gy, gz = fields.shape[1:]
    k = nbx * 128
    dma = pltpu.SemaphoreType.DMA
    wide = (gx + 2 * WIDE, gy + 2 * PAD, gz)
    kept = ((gx, gy, gz), (gx + 2 * REACH, gy, gz), (gx, gy + 2 * PAD, gz), (gx, gy, gz))
    sems = (9, 4, 12, 12, nby, nby, nbx, nbx, 4, 4, 4, 4)
    state = pl.pallas_call(
        functools.partial(box_kernel, nbx, nby),
        out_shape=[jax.ShapeDtypeStruct(shape, F32) for shape in kept],
        in_specs=[pl.BlockSpec(memory_space=pltpu.HBM)] * 10,
        out_specs=[vmem()] * 4,
        scratch_shapes=[
            pltpu.VMEM(wide, F32),
            pltpu.VMEM(wide, F32),
            pltpu.VMEM((gx, gy, gz), F32),
            pltpu.VMEM((3 * gz, 2 * gz), BF),
            pltpu.VMEM((gx * gy, k), BF),
            pltpu.VMEM((2, WIDE * gy, k), BF),
            pltpu.VMEM((2, gx * PAD, k), BF),
            pltpu.VMEM((2, 2 * gz, k), BF),
            pltpu.VMEM((nby, nbx, 128), F32),
            pltpu.VMEM((nbx, 1, 128), F32),
            pltpu.VMEM((nbx, 1, 128), F32),
            pltpu.VMEM((4, nbx, 1, 128), F32),
            pltpu.VMEM((4, nbx, 128), jnp.int32),
            pltpu.VMEM((3, m), F32),
            pltpu.VMEM((1, m), jnp.int32),
            pltpu.VMEM((1, m), F32),
            pltpu.VMEM((1, m), jnp.int32),
            pltpu.VMEM((3, q), F32),
            pltpu.VMEM((3, q), F32),
            pltpu.VMEM((3, sources.shape[2], q), BF),
            pltpu.VMEM((nbx, 128), jnp.int32),
            pltpu.VMEM((gx, gy), jnp.int32),
            pltpu.VMEM((devices, 128), F32),
        ] + panel_scratch(m, q, devices) + [dma((n,)) for n in sems],
        compiler_params=pltpu.CompilerParams(
            collective_id=0, has_side_effects=True, vmem_limit_bytes=44 << 20
        ),
        name="box",
    )(*[pltpu.with_memory_space_constraint(v, pltpu.HBM) for v in (
        observers,
        slots.reshape(1, m),
        fractions.reshape(1, m),
        owners.reshape(1, m),
        panel_points,
        panel_normals,
        sources.transpose(0, 2, 1),
        arrival_cell,
        ground,
        fields,
    )])
    return pl.pallas_call(
        last_kernel,
        out_shape=jax.ShapeDtypeStruct(fields.shape, F32),
        in_specs=[vmem()] * 4,
        out_specs=anywhere(),
        scratch_shapes=[pltpu.VMEM((gx, gy, gz), F32), dma((3 + gx // min(8, gx),))],
        compiler_params=pltpu.CompilerParams(vmem_limit_bytes=8 << 20),
        name="last",
    )(*state)


def solution(mesh):
    placed = (
        P(None, "bx", "by", None),
        P("bx", "by"),
        P(None, "bx"),
        P("bx"),
        P("bx"),
        P("bx", None),
        P(("bx", "by"), None, None),
        P(None, "by"),
        P(None, "by"),
        P(None, "by", None),
    )
    return jax.shard_map(
        functools.partial(body, mesh.shape["bx"], mesh.shape["by"]),
        mesh=mesh,
        in_specs=placed,
        out_specs=P(None, "bx", "by", None),
        check_vma=False,
    )
```

```python
import functools

import jax
import jax.numpy as jnp
from jax import lax
from jax.experimental import pallas as pl
from jax.experimental.pallas import tpu as pltpu
from jax.sharding import PartitionSpec as P

BF = jnp.bfloat16
F32 = jnp.float32
MESH = pl.DeviceIdType.MESH
WEIGHTS = (0.770882380518, -0.166705904415, 0.02084314277)
DT = 0.5
SOFTENING = 0.01
REACH = 3
WIDE = 6
PAD = 8
FEATURES = 80


def split3(x):
    a = x.astype(BF).astype(F32)
    r = x - a
    b = r.astype(BF).astype(F32)
    return a, b, r - b


def dot(a, b):
    return jnp.dot(a, b, preferred_element_type=F32)


def dot_nt(a, b):
    return lax.dot_general(a, b, (((1,), (1,)), ((), ())), preferred_element_type=F32)


def panel_scratch(m, q, devices):
    return [
        pltpu.VMEM((8, m), F32),
        pltpu.VMEM((8, q), F32),
        pltpu.VMEM((2, q, FEATURES), BF),
        pltpu.VMEM((3 * devices, 128), F32),
        pltpu.VMEM((devices, 128), F32),
    ]


def panel_part(nbx, nby, obs, slots, fracs, owners, pts, nrm, src, packet, eo, ep, feat, pieces, base, kern, ready):
    m = obs.shape[1]
    q = pts.shape[1]
    samples = src.shape[1]
    devices = nbx * nby
    tile = min(1024, m, kern.shape[1])
    chunk = min(512, q)
    sub = 256
    block = 256

    o = obs[...]
    eo[0:3, :] = o
    eo[3:4, :] = jnp.sum(o * o, axis=0, keepdims=True)
    eo[4:5, :] = jnp.ones((1, m), F32)
    eo[5:8, :] = jnp.zeros((3, m), F32)
    p = pts[...]
    n = nrm[...]

    def lay(k):
        s = split3(ep[...])
        rows = [s[0], s[1], s[2]] * 3 + [jnp.zeros_like(s[0])]
        table = jnp.concatenate(rows + [jnp.zeros((128 - FEATURES, q), F32)], axis=0)
        feat[k] = table.T[:, :FEATURES].astype(BF)

    ep[0:3, :] = -2.0 * p
    ep[3:4, :] = jnp.ones((1, q), F32)
    ep[4:5, :] = jnp.sum(p * p, axis=0, keepdims=True) + SOFTENING
    ep[5:8, :] = jnp.zeros((3, q), F32)
    lay(0)
    ep[0:3, :] = n
    ep[3:4, :] = jnp.zeros((1, q), F32)
    ep[4:5, :] = -jnp.sum(p * n, axis=0, keepdims=True)
    lay(1)
    ready()
    pieces[...] = jnp.zeros_like(pieces)
    base[...] = jnp.zeros_like(base)
    row = lax.broadcasted_iota(jnp.int32, (devices, 1), 0)
    row_owner = (row % nbx) * nby + row // nbx
    before = (
        lax.broadcasted_iota(jnp.int32, (sub, sub), 0) < lax.broadcasted_iota(jnp.int32, (sub, sub), 1)
    ).astype(F32).astype(BF)
    ranks = lax.broadcasted_iota(jnp.int32, (128, 1), 0).astype(F32)
    times = lax.broadcasted_iota(jnp.int32, (samples, 1), 0)

    def one_tile(t, carry):
        o0 = pl.multiple_of(t * tile, tile)
        here = pl.ds(o0, tile)
        e = split3(eo[:, here])
        of = jnp.concatenate(
            [e[0]] * 3 + [e[1]] * 3 + [e[2]] * 3 + [jnp.zeros_like(e[0])], axis=0
        ).astype(BF)

        def one_chunk(c, acc):
            q0 = pl.multiple_of(c * chunk, chunk)
            rows = pl.ds(q0, chunk)
            for l in range(0, tile, block):
                wide = slice(l, l + block)
                for r in range(0, chunk, block):
                    some = pl.ds(q0 + r, block)
                    inverse = lax.rsqrt(dot(feat[0, some, :], of[:, wide]))
                    near = dot(feat[1, some, :], of[:, wide]) * inverse * inverse
                    kern[r:r + block, wide] = inverse.astype(BF)
                    kern[chunk + r:chunk + r + block, wide] = near.astype(BF)
                    kern[2 * chunk + r:2 * chunk + r + block, wide] = (near * inverse).astype(BF)
            for k in range(3):
                acc = acc + dot(src[k, :, rows], kern[k * chunk:(k + 1) * chunk, 0:tile])
            return acc

        history = lax.fori_loop(0, q // chunk, one_chunk, jnp.zeros((samples, tile), F32))
        slot = slots[:, here]
        frac = fracs[:, here]
        weights = jnp.where(times == slot, 1.0 - frac, 0.0) + jnp.where(times == slot + 1, frac, 0.0)
        value = jnp.sum(history * weights, axis=0, keepdims=True)
        parts = split3(value)
        owner = owners[:, here]
        mine = owner == row_owner
        hot = jnp.where(mine, 1.0, 0.0)
        seen = base[...]
        ranks_here = []
        for s in range(tile // sub):
            part = hot[:, s * sub:(s + 1) * sub]
            earlier = dot(part.astype(BF), before) + seen[:, 0:1]
            ranks_here.append(jnp.sum(part * earlier, axis=0, keepdims=True))
            seen = seen + jnp.sum(part, axis=1, keepdims=True)
        base[...] = seen
        rank = jnp.concatenate(ranks_here, axis=1)
        at_rank = jnp.where(rank == ranks, 1.0, 0.0).astype(BF)
        loads = jnp.concatenate([jnp.where(mine, v, 0.0) for v in parts], axis=0).astype(BF)
        pieces[...] += dot_nt(loads, at_rank)
        return carry

    lax.fori_loop(0, m // tile, one_tile, 0)
    packet[...] = pieces[0:devices, :] + pieces[devices:2 * devices, :] + pieces[2 * devices:, :]


def box_kernel(nbx, nby, obs_in, slots_in, fracs_in, owners_in, pts_in, nrm_in, src_in, cells_in, ground_in, fields,
               pz, us, vs, ws, pa, pb, flags, zmat, hot_own, hot_lr, hot_du, bt,
               gathered, agg, arrived, passed, passed_cells, obs, slots, fracs, owners, pts, nrm, src, cells, ground,
               packet, eo, ep, feat, pieces, base, in_sem, load_sem, raw_send, raw_recv, one_send, one_recv,
               two_send, two_recv, nb_send, nb_recv, rim_send, rim_recv):
    bx = lax.axis_index("bx")
    by = lax.axis_index("by")
    gx, gy, gz = fields.shape[1:]
    arrivals = nbx * 128
    has = (bx > 0, bx < nbx - 1, by > 0, by < nby - 1)
    to = (
        (jnp.maximum(bx - 1, 0), by),
        (jnp.minimum(bx + 1, nbx - 1), by),
        (bx, jnp.maximum(by - 1, 0)),
        (bx, jnp.minimum(by + 1, nby - 1)),
    )
    back = (1, 0, 3, 2)

    fetched = [
        pltpu.make_async_copy(a, b, in_sem.at[i])
        for i, (a, b) in enumerate((
            (cells_in.at[0], cells), (ground_in, ground), (src_in, src), (obs_in, obs), (slots_in, slots),
            (fracs_in, fracs), (owners_in, owners), (pts_in, pts), (nrm_in, nrm),
        ))
    ]
    for copy in fetched:
        copy.start()
    barrier = pltpu.get_barrier_semaphore()
    for i in range(1, nby):
        pl.semaphore_signal(barrier, inc=1, device_id=(bx, lax.rem(by + i, nby)), device_id_type=MESH)
    for i in range(1, nbx):
        pl.semaphore_signal(barrier, inc=1, device_id=(lax.rem(bx + i, nbx), by), device_id_type=MESH)

    def remote(src, dst, send, recv, target):
        return pltpu.make_async_remote_copy(
            src_ref=src, dst_ref=dst, send_sem=send, recv_sem=recv, device_id=target, device_id_type=MESH
        )

    x_core = pl.ds(WIDE, gx)
    y_core = pl.ds(PAD, gy)
    give_p = (
        fields.at[0, pl.ds(0, WIDE)],
        fields.at[0, pl.ds(gx - WIDE, WIDE)],
        fields.at[0, :, pl.ds(0, PAD)],
        fields.at[0, :, pl.ds(gy - PAD, PAD)],
    )
    give_v = (
        fields.at[1, pl.ds(0, REACH)],
        fields.at[1, pl.ds(gx - REACH, REACH)],
        fields.at[2, :, pl.ds(0, PAD)],
        fields.at[2, :, pl.ds(gy - PAD, PAD)],
    )

    def rim(ref):
        return (
            ref.at[pl.ds(0, WIDE), y_core],
            ref.at[pl.ds(WIDE + gx, WIDE), y_core],
            ref.at[x_core, pl.ds(0, PAD)],
            ref.at[x_core, pl.ds(PAD + gy, PAD)],
        )

    rim_a = rim(pa)
    rim_b = rim(pb)
    rim_v = (
        us.at[pl.ds(0, REACH)],
        us.at[pl.ds(REACH + gx, REACH)],
        vs.at[:, pl.ds(0, PAD)],
        vs.at[:, pl.ds(PAD + gy, PAD)],
    )

    raw = []
    for s in range(4):
        raw.append((
            remote(cells_in.at[0], passed_cells.at[back[s]], raw_send.at[s], raw_recv.at[s], to[s]),
            remote(give_p[s], rim_a[back[s]], raw_send.at[4 + s], raw_recv.at[4 + s], to[s]),
            remote(give_v[s], rim_v[back[s]], raw_send.at[8 + s], raw_recv.at[8 + s], to[s]),
        ))

    def landed(src, dst, recv, s):
        return remote(src, dst, raw_send.at[s], recv, to[s % 4])

    loads = [
        pltpu.make_async_copy(fields.at[0], pa.at[x_core, y_core], load_sem.at[0]),
        pltpu.make_async_copy(fields.at[1], us.at[pl.ds(REACH, gx)], load_sem.at[1]),
        pltpu.make_async_copy(fields.at[2], vs.at[:, y_core], load_sem.at[2]),
        pltpu.make_async_copy(fields.at[3], ws, load_sem.at[3]),
    ]
    for copy in loads:
        copy.start()

    for s in range(4):
        @pl.when(jnp.logical_not(has[s]))
        def _(s=s):
            rim_a[s][...] = jnp.zeros(rim_a[s].shape, F32)
            rim_b[s][...] = jnp.zeros(rim_b[s].shape, F32)
            rim_v[s][...] = jnp.zeros(rim_v[s].shape, F32)

    scaled = [DT * w for w in WEIGHTS]
    source = lax.broadcasted_iota(jnp.int32, (gz, 2 * gz), 0)
    column = lax.broadcasted_iota(jnp.int32, (gz, 2 * gz), 1)
    difference = jnp.zeros((gz, 2 * gz), F32)
    for j, w in enumerate(scaled, 1):
        difference = jnp.where(jnp.logical_and(column < gz, source - column == j), w, difference)
        difference = jnp.where(jnp.logical_and(column < gz, column - source == j), -w, difference)
        difference = jnp.where(jnp.logical_and(column >= gz, source + column - gz + 1 == j), -w, difference)
    coarse = difference.astype(BF)
    zmat[0:gz, :] = coarse
    zmat[gz:2 * gz, :] = coarse
    zmat[2 * gz:, :] = (difference - coarse.astype(F32)).astype(BF)

    for copy in fetched:
        copy.wait()
    ground_t = ground[...].astype(F32).T
    for x in range(gx):
        flags[x] = jnp.broadcast_to(ground_t[:, x:x + 1], (gy, gz))

    def greet_and_send():
        pl.semaphore_wait(barrier, nby - 1 + nbx - 1)
        for s in range(4):
            @pl.when(has[s])
            def _(s=s):
                for copy in raw[s]:
                    copy.start()


    panel_part(nbx, nby, obs, slots, fracs, owners, pts, nrm, src, packet, eo, ep, feat, pieces, base,
               hot_own, greet_and_send)
    firsts = []
    for i in range(1, nby):
        peer = lax.rem(by + i, nby)
        rows = pl.ds(pl.multiple_of(peer * nbx, nbx), nbx)
        copy = remote(packet.at[rows, :], gathered.at[i], one_send.at[i], one_recv.at[i], (bx, peer))
        copy.start()
        firsts.append(copy)

    def fill(ref, rows, row_id):
        step = min(256, rows)

        def go(i, carry):
            r0 = pl.multiple_of(i * step, step)
            ids = lax.broadcasted_iota(jnp.int32, (step, 1), 0) + r0
            for b in range(nbx):
                ref[pl.ds(r0, step), b * 128:(b + 1) * 128] = jnp.where(
                    ids == row_id[b:b + 1, :], 1.0, 0.0
                ).astype(BF)
            return carry

        lax.fori_loop(0, rows // step, go, 0)

    fill(hot_own, gx * gy, cells[...] // gz)

    for copy in firsts:
        copy.wait_recv()
    mine = pl.ds(pl.multiple_of(by * nbx, nbx), nbx)
    total = packet[mine, :]
    for i in range(1, nby):
        total = total + gathered[i]
    for i in range(nbx):
        agg[i] = total[i:i + 1, :]
    seconds = []
    for i in range(1, nbx):
        peer = lax.rem(bx + i, nbx)
        copy = remote(agg.at[peer], arrived.at[bx], two_send.at[i], two_recv.at[i], (peer, by))
        copy.start()
        seconds.append(copy)
    arrived[bx] = agg[bx]

    for s in range(4):
        @pl.when(has[s])
        def _(s=s):
            landed(cells_in.at[0], passed_cells.at[s], raw_recv.at[back[s]], s).wait_recv()
            row_id = passed_cells[s] // gz
            if s == 0:
                fill(hot_lr.at[0], WIDE * gy, row_id - (gx - WIDE) * gy)
            elif s == 1:
                fill(hot_lr.at[1], WIDE * gy, row_id)
            else:
                y = row_id % gy - (gy - PAD if s == 2 else 0)
                inside = jnp.logical_and(y >= 0, y < PAD)
                fill(hot_du.at[s - 2], gx * PAD, jnp.where(inside, row_id // gy * PAD + y, -1))

    heights = lax.broadcasted_iota(jnp.int32, (gz, 1), 0)

    def targets(bt, values, cell_rows):
        for b in range(nbx):
            v = values(b)
            at = heights == cell_rows[b:b + 1, :] % gz
            hi = v.astype(BF).astype(F32)
            bt[0:gz, b * 128:(b + 1) * 128] = jnp.where(at, hi, 0.0).astype(BF)
            bt[gz:2 * gz, b * 128:(b + 1) * 128] = jnp.where(at, v - hi, 0.0).astype(BF)

    def added(hot, bt):
        both = dot_nt(hot, bt[...])
        return both[:, :gz] + both[:, gz:]

    for copy in seconds:
        copy.wait_recv()
    handed = [
        remote(arrived, passed.at[back[s]], nb_send.at[s], nb_recv.at[s], to[s]) for s in range(4)
    ]
    for s in range(4):
        @pl.when(has[s])
        def _(s=s):
            handed[s].start()

    own, theirs = bt.at[0], bt.at[1]
    targets(own, lambda b: arrived[b], cells[...])
    loads[0].wait()
    planes = min(4, gx)
    ends = 2
    near = min(2 * WIDE, gx // 2)

    def inject_own(lo, hi):
        count = hi - lo
        step = next(n for n in (6, 4, 2, 1) if count % n == 0)

        def go(i, carry):
            x = lo + i * step
            rows = pl.ds(pl.multiple_of(x * gy, gy), step * gy)
            pa[pl.ds(WIDE + x, step), PAD:PAD + gy, :] += added(hot_own[rows, :], own).reshape(step, gy, gz)
            return carry

        lax.fori_loop(0, count // step, go, 0)

    inject_own(0, near)
    inject_own(gx - near, gx)

    for s in range(4):
        @pl.when(has[s])
        def _(s=s):
            landed(give_p[s], rim_a[s], raw_recv.at[4 + back[s]], 4 + s).wait_recv()
            landed(give_v[s], rim_v[s], raw_recv.at[8 + back[s]], 8 + s).wait_recv()
            remote(arrived, passed.at[s], nb_send.at[s], nb_recv.at[back[s]], to[s]).wait_recv()
            targets(theirs, lambda b: passed[s, b], passed_cells[s])
            if s < 2:
                x0 = 0 if s == 0 else WIDE + gx
                pa[x0:x0 + WIDE, PAD:PAD + gy, :] += added(hot_lr[s], theirs).reshape(WIDE, gy, gz)
            else:
                y0 = 0 if s == 2 else PAD + gy
                pa[WIDE:WIDE + gx, y0:y0 + PAD, :] += added(hot_du[s - 2], theirs).reshape(gx, PAD, gz)

    for copy in loads[1:]:
        copy.wait()

    def z_term(f, flag):
        high = f.astype(BF)
        low = (f - high.astype(F32)).astype(BF)
        both = dot(jnp.concatenate([high, low, high], axis=1), zmat[...])
        return both[:, :gz] + flag * both[:, gz:]

    def span(get):
        total = None
        for j, w in enumerate(scaled, 1):
            term = w * (get(j) - get(-j))
            total = term if total is None else total + term
        return total

    def loop(lo, hi, step):
        def go(i, carry):
            step(i)
            return carry

        lax.fori_loop(lo, hi, go, 0)

    def u_plane(p, i):
        us[i] = us[i] - span(lambda j: p[i + REACH + j, PAD:PAD + gy, :])

    def v_rows(p, x, lo, hi):
        vs[x, lo:hi, :] = vs[x, lo:hi, :] - span(lambda j: p[x + WIDE, lo + j:hi + j, :])

    def w_planes(p, new, x, shift):
        rows = planes * gy
        shift_y = PAD if shift else 0
        f = p[pl.ds(x + WIDE, planes), PAD:PAD + gy, :].reshape(rows, gz)
        flag = flags[pl.ds(x, planes)].reshape(rows, gz)
        w = ws[pl.ds(x, planes)].reshape(rows, gz) - z_term(f, flag)
        ws[pl.ds(x, planes)] = w.reshape(planes, gy, gz)
        new[pl.ds(x + shift, planes), shift_y:shift_y + gy, :] = (f - z_term(w, -flag)).reshape(planes, gy, gz)

    def p_rows(p, x, lo, hi):
        change = span(lambda j: us[x + REACH + j, lo:hi, :])
        change = change + span(lambda j: vs[x, PAD + lo + j:PAD + hi + j, :])
        p[x + WIDE, PAD + lo:PAD + hi, :] = p[x + WIDE, PAD + lo:PAD + hi, :] - change

    def outer_u(p, s):
        lo = 0 if s == 0 else REACH + gx

        @pl.when(has[s])
        def _():
            loop(lo, lo + REACH, lambda i: u_plane(p, i))

    def outer_v(p, s, x0, x1):
        lo = PAD - REACH if s == 2 else PAD + gy

        @pl.when(has[s])
        def _():
            loop(x0, x1, lambda x: v_rows(p, x, lo, lo + REACH))

    for s in (0, 1):
        outer_u(pa, s)
    for s in (2, 3):
        outer_v(pa, s, 0, WIDE)
        outer_v(pa, s, gx - WIDE, gx)

    few = min(WIDE + REACH, gx // 2)
    loop(REACH, REACH + few, lambda i: u_plane(pa, i))
    loop(REACH + gx - few, REACH + gx, lambda i: u_plane(pa, i))
    loop(0, WIDE, lambda x: v_rows(pa, x, PAD, PAD + gy))
    loop(gx - WIDE, gx, lambda x: v_rows(pa, x, PAD, PAD + gy))
    third = gx // planes - 2 * ends

    def w_blocks(p, new, lo, hi, shift):
        loop(lo, hi, lambda i: w_planes(p, new, i * planes, shift))

    w_blocks(pa, pb, 0, ends, WIDE)
    w_blocks(pa, pb, ends + third, 2 * ends + third, WIDE)

    give_b = (
        pb.at[pl.ds(WIDE, WIDE), y_core],
        pb.at[pl.ds(gx, WIDE), y_core],
        pb.at[x_core, pl.ds(PAD, PAD)],
        pb.at[x_core, pl.ds(gy, PAD)],
    )
    second_rim = [
        remote(give_b[s], rim_b[back[s]], rim_send.at[s], rim_recv.at[s], to[s]) for s in range(4)
    ]

    def send_rim(s):
        @pl.when(has[s])
        def _():
            second_rim[s].start()

    loop(0, WIDE, lambda x: p_rows(pb, x, 0, gy))
    send_rim(0)
    loop(gx - WIDE, gx, lambda x: p_rows(pb, x, 0, gy))
    send_rim(1)
    if gx > 2 * near:
        inject_own(near, gx - near)
    for s in (2, 3):
        outer_v(pa, s, WIDE, gx - WIDE)
    loop(WIDE, gx - WIDE, lambda x: v_rows(pa, x, PAD, PAD + gy))
    w_blocks(pa, pb, ends, ends + third, WIDE)
    loop(REACH + few, REACH + gx - few, lambda i: u_plane(pa, i))

    def edges(x):
        p_rows(pb, x, 0, PAD)
        p_rows(pb, x, gy - PAD, gy)

    loop(WIDE, gx - WIDE, edges)
    send_rim(2)
    send_rim(3)
    loop(WIDE, gx - WIDE, lambda x: p_rows(pb, x, PAD, gy - PAD))

    w_blocks(pb, pz, 0, gx // planes, 0)
    loop(0, gx, lambda x: v_rows(pb, x, 2 * PAD, gy))
    loop(2 * REACH, gx, lambda i: u_plane(pb, i))
    for s in range(4):
        @pl.when(has[s])
        def _(s=s):
            remote(give_b[s], rim_b[s], rim_send.at[s], rim_recv.at[back[s]], to[s]).wait_recv()
    for s in (0, 1):
        outer_u(pb, s)
    loop(REACH, 2 * REACH, lambda i: u_plane(pb, i))
    loop(gx, gx + REACH, lambda i: u_plane(pb, i))
    for s in (2, 3):
        outer_v(pb, s, 0, gx)

    def outer_rows(x):
        v_rows(pb, x, PAD, 2 * PAD)
        v_rows(pb, x, gy, gy + PAD)

    loop(0, gx, outer_rows)

    for copy in firsts + seconds:
        copy.wait_send()
    for s in range(4):
        @pl.when(has[s])
        def _(s=s):
            for copy in raw[s]:
                copy.wait_send()
            handed[s].wait_send()
            second_rim[s].wait_send()


def last_kernel(pz, us, vs, ws, out, held, sems):
    gx, gy, gz = ws.shape
    step = min(8, gx)
    copies = [
        pltpu.make_async_copy(us.at[pl.ds(REACH, gx)], out.at[1], sems.at[0]),
        pltpu.make_async_copy(vs.at[:, pl.ds(PAD, gy)], out.at[2], sems.at[1]),
        pltpu.make_async_copy(ws, out.at[3], sems.at[2]),
    ]
    for copy in copies:
        copy.start()
    for part in range(gx // step):
        def plane(i, carry):
            x = part * step + i
            change = None
            for j, w in enumerate(WEIGHTS, 1):
                term = (DT * w) * (
                    us[x + REACH + j] - us[x + REACH - j]
                    + (vs[x, PAD + j:PAD + gy + j, :] - vs[x, PAD - j:PAD + gy - j, :])
                )
                change = term if change is None else change + term
            held[x] = pz[x] - change
            return carry

        lax.fori_loop(0, step, plane, 0)
        rows = pl.ds(part * step, step)
        copy = pltpu.make_async_copy(held.at[rows], out.at[0, rows], sems.at[3 + part])
        copy.start()
        copies.append(copy)
    for copy in copies:
        copy.wait()


def vmem():
    return pl.BlockSpec(memory_space=pltpu.VMEM)


def anywhere():
    return pl.BlockSpec(memory_space=pl.ANY)


def body(nbx, nby, fields, ground, observers, slots, fractions, owners, arrival_cell, panel_points, panel_normals,
         sources):
    devices = nbx * nby
    m = observers.shape[1]
    q = panel_points.shape[1]
    gx, gy, gz = fields.shape[1:]
    k = nbx * 128
    dma = pltpu.SemaphoreType.DMA
    wide = (gx + 2 * WIDE, gy + 2 * PAD, gz)
    kept = ((gx, gy, gz), (gx + 2 * REACH, gy, gz), (gx, gy + 2 * PAD, gz), (gx, gy, gz))
    sems = (9, 4, 12, 12, nby, nby, nbx, nbx, 4, 4, 4, 4)
    state = pl.pallas_call(
        functools.partial(box_kernel, nbx, nby),
        out_shape=[jax.ShapeDtypeStruct(shape, F32) for shape in kept],
        in_specs=[pl.BlockSpec(memory_space=pltpu.HBM)] * 10,
        out_specs=[vmem()] * 4,
        scratch_shapes=[
            pltpu.VMEM(wide, F32),
            pltpu.VMEM(wide, F32),
            pltpu.VMEM((gx, gy, gz), F32),
            pltpu.VMEM((3 * gz, 2 * gz), BF),
            pltpu.VMEM((gx * gy, k), BF),
            pltpu.VMEM((2, WIDE * gy, k), BF),
            pltpu.VMEM((2, gx * PAD, k), BF),
            pltpu.VMEM((2, 2 * gz, k), BF),
            pltpu.VMEM((nby, nbx, 128), F32),
            pltpu.VMEM((nbx, 1, 128), F32),
            pltpu.VMEM((nbx, 1, 128), F32),
            pltpu.VMEM((4, nbx, 1, 128), F32),
            pltpu.VMEM((4, nbx, 128), jnp.int32),
            pltpu.VMEM((3, m), F32),
            pltpu.VMEM((1, m), jnp.int32),
            pltpu.VMEM((1, m), F32),
            pltpu.VMEM((1, m), jnp.int32),
            pltpu.VMEM((3, q), F32),
            pltpu.VMEM((3, q), F32),
            pltpu.VMEM((3, sources.shape[2], q), BF),
            pltpu.VMEM((nbx, 128), jnp.int32),
            pltpu.VMEM((gx, gy), jnp.int32),
            pltpu.VMEM((devices, 128), F32),
        ] + panel_scratch(m, q, devices) + [dma((n,)) for n in sems],
        compiler_params=pltpu.CompilerParams(
            collective_id=0, has_side_effects=True, vmem_limit_bytes=44 << 20
        ),
        name="box",
    )(*[pltpu.with_memory_space_constraint(v, pltpu.HBM) for v in (
        observers,
        slots.reshape(1, m),
        fractions.reshape(1, m),
        owners.reshape(1, m),
        panel_points,
        panel_normals,
        sources.transpose(0, 2, 1),
        arrival_cell,
        ground,
        fields,
    )])
    return pl.pallas_call(
        last_kernel,
        out_shape=jax.ShapeDtypeStruct(fields.shape, F32),
        in_specs=[vmem()] * 4,
        out_specs=anywhere(),
        scratch_shapes=[pltpu.VMEM((gx, gy, gz), F32), dma((3 + gx // min(8, gx),))],
        compiler_params=pltpu.CompilerParams(vmem_limit_bytes=8 << 20),
        name="last",
    )(*state)


def solution(mesh):
    placed = (
        P(None, "bx", "by", None),
        P("bx", "by"),
        P(None, "bx"),
        P("bx"),
        P("bx"),
        P("bx", None),
        P(("bx", "by"), None, None),
        P(None, "by"),
        P(None, "by"),
        P(None, "by", None),
    )
    return jax.shard_map(
        functools.partial(body, mesh.shape["bx"], mesh.shape["by"]),
        mesh=mesh,
        in_specs=placed,
        out_specs=P(None, "bx", "by", None),
        check_vma=False,
    )
```

```python
import functools

import jax
import jax.numpy as jnp
from jax import lax
from jax.experimental import pallas as pl
from jax.experimental.pallas import tpu as pltpu
from jax.sharding import PartitionSpec as P

BF = jnp.bfloat16
F32 = jnp.float32
MESH = pl.DeviceIdType.MESH
WEIGHTS = (0.770882380518, -0.166705904415, 0.02084314277)
DT = 0.5
SOFTENING = 0.01
REACH = 3
WIDE = 6
PAD = 8
FEATURES = 80


def split3(x):
    a = x.astype(BF).astype(F32)
    r = x - a
    b = r.astype(BF).astype(F32)
    return a, b, r - b


def dot(a, b):
    return jnp.dot(a, b, preferred_element_type=F32)


def dot_nt(a, b):
    return lax.dot_general(a, b, (((1,), (1,)), ((), ())), preferred_element_type=F32)


def panel_scratch(m, q, devices):
    return [
        pltpu.VMEM((8, m), F32),
        pltpu.VMEM((8, q), F32),
        pltpu.VMEM((2, q, FEATURES), BF),
        pltpu.VMEM((3 * devices, 128), F32),
        pltpu.VMEM((devices, 128), F32),
    ]


def panel_part(nbx, nby, obs, slots, fracs, owners, pts, nrm, src, packet, eo, ep, feat, pieces, base, kern, ready):
    m = obs.shape[1]
    q = pts.shape[1]
    samples = src.shape[1]
    devices = nbx * nby
    tile = min(1024, m, kern.shape[1])
    chunk = min(512, q)
    sub = 256
    block = 256

    o = obs[...]
    eo[0:3, :] = o
    eo[3:4, :] = jnp.sum(o * o, axis=0, keepdims=True)
    eo[4:5, :] = jnp.ones((1, m), F32)
    eo[5:8, :] = jnp.zeros((3, m), F32)
    p = pts[...]
    n = nrm[...]

    def lay(k):
        s = split3(ep[...])
        rows = [s[0], s[1], s[2]] * 3 + [jnp.zeros_like(s[0])]
        table = jnp.concatenate(rows + [jnp.zeros((128 - FEATURES, q), F32)], axis=0)
        feat[k] = table.T[:, :FEATURES].astype(BF)

    ep[0:3, :] = -2.0 * p
    ep[3:4, :] = jnp.ones((1, q), F32)
    ep[4:5, :] = jnp.sum(p * p, axis=0, keepdims=True) + SOFTENING
    ep[5:8, :] = jnp.zeros((3, q), F32)
    lay(0)
    ep[0:3, :] = n
    ep[3:4, :] = jnp.zeros((1, q), F32)
    ep[4:5, :] = -jnp.sum(p * n, axis=0, keepdims=True)
    lay(1)
    ready()
    pieces[...] = jnp.zeros_like(pieces)
    base[...] = jnp.zeros_like(base)
    row = lax.broadcasted_iota(jnp.int32, (devices, 1), 0)
    row_owner = (row % nbx) * nby + row // nbx
    before = (
        lax.broadcasted_iota(jnp.int32, (sub, sub), 0) < lax.broadcasted_iota(jnp.int32, (sub, sub), 1)
    ).astype(F32).astype(BF)
    ranks = lax.broadcasted_iota(jnp.int32, (128, 1), 0).astype(F32)
    times = lax.broadcasted_iota(jnp.int32, (samples, 1), 0)

    def one_tile(t, carry):
        o0 = pl.multiple_of(t * tile, tile)
        here = pl.ds(o0, tile)
        e = split3(eo[:, here])
        of = jnp.concatenate(
            [e[0]] * 3 + [e[1]] * 3 + [e[2]] * 3 + [jnp.zeros_like(e[0])], axis=0
        ).astype(BF)

        def one_chunk(c, acc):
            q0 = pl.multiple_of(c * chunk, chunk)
            rows = pl.ds(q0, chunk)
            for l in range(0, tile, block):
                wide = slice(l, l + block)
                for r in range(0, chunk, block):
                    some = pl.ds(q0 + r, block)
                    inverse = lax.rsqrt(dot(feat[0, some, :], of[:, wide]))
                    near = dot(feat[1, some, :], of[:, wide]) * inverse * inverse
                    kern[r:r + block, wide] = inverse.astype(BF)
                    kern[chunk + r:chunk + r + block, wide] = near.astype(BF)
                    kern[2 * chunk + r:2 * chunk + r + block, wide] = (near * inverse).astype(BF)
            for k in range(3):
                acc = acc + dot(src[k, :, rows], kern[k * chunk:(k + 1) * chunk, 0:tile])
            return acc

        history = lax.fori_loop(0, q // chunk, one_chunk, jnp.zeros((samples, tile), F32))
        slot = slots[:, here]
        frac = fracs[:, here]
        weights = jnp.where(times == slot, 1.0 - frac, 0.0) + jnp.where(times == slot + 1, frac, 0.0)
        value = jnp.sum(history * weights, axis=0, keepdims=True)
        parts = split3(value)
        owner = owners[:, here]
        mine = owner == row_owner
        hot = jnp.where(mine, 1.0, 0.0)
        seen = base[...]
        ranks_here = []
        for s in range(tile // sub):
            part = hot[:, s * sub:(s + 1) * sub]
            earlier = dot(part.astype(BF), before) + seen[:, 0:1]
            ranks_here.append(jnp.sum(part * earlier, axis=0, keepdims=True))
            seen = seen + jnp.sum(part, axis=1, keepdims=True)
        base[...] = seen
        rank = jnp.concatenate(ranks_here, axis=1)
        at_rank = jnp.where(rank == ranks, 1.0, 0.0).astype(BF)
        loads = jnp.concatenate([jnp.where(mine, v, 0.0) for v in parts], axis=0).astype(BF)
        pieces[...] += dot_nt(loads, at_rank)
        return carry

    lax.fori_loop(0, m // tile, one_tile, 0)
    packet[...] = pieces[0:devices, :] + pieces[devices:2 * devices, :] + pieces[2 * devices:, :]


def box_kernel(nbx, nby, obs_in, slots_in, fracs_in, owners_in, pts_in, nrm_in, src_in, cells_in, ground_in, fields,
               pz, us, vs, ws, pa, pb, flags, zmat, hot_own, hot_lr, hot_du, bt,
               gathered, agg, arrived, passed, passed_cells, obs, slots, fracs, owners, pts, nrm, src, cells, ground,
               packet, eo, ep, feat, pieces, base, in_sem, load_sem, raw_send, raw_recv, one_send, one_recv,
               two_send, two_recv, nb_send, nb_recv, rim_send, rim_recv):
    bx = lax.axis_index("bx")
    by = lax.axis_index("by")
    gx, gy, gz = fields.shape[1:]
    arrivals = nbx * 128
    has = (bx > 0, bx < nbx - 1, by > 0, by < nby - 1)
    to = (
        (jnp.maximum(bx - 1, 0), by),
        (jnp.minimum(bx + 1, nbx - 1), by),
        (bx, jnp.maximum(by - 1, 0)),
        (bx, jnp.minimum(by + 1, nby - 1)),
    )
    back = (1, 0, 3, 2)

    fetched = [
        pltpu.make_async_copy(a, b, in_sem.at[i])
        for i, (a, b) in enumerate((
            (cells_in.at[0], cells), (ground_in, ground), (src_in, src), (obs_in, obs), (slots_in, slots),
            (fracs_in, fracs), (owners_in, owners), (pts_in, pts), (nrm_in, nrm),
        ))
    ]
    for copy in fetched:
        copy.start()
    barrier = pltpu.get_barrier_semaphore()
    for i in range(1, nby):
        pl.semaphore_signal(barrier, inc=1, device_id=(bx, lax.rem(by + i, nby)), device_id_type=MESH)
    for i in range(1, nbx):
        pl.semaphore_signal(barrier, inc=1, device_id=(lax.rem(bx + i, nbx), by), device_id_type=MESH)

    def remote(src, dst, send, recv, target):
        return pltpu.make_async_remote_copy(
            src_ref=src, dst_ref=dst, send_sem=send, recv_sem=recv, device_id=target, device_id_type=MESH
        )

    x_core = pl.ds(WIDE, gx)
    y_core = pl.ds(PAD, gy)
    give_p = (
        fields.at[0, pl.ds(0, WIDE)],
        fields.at[0, pl.ds(gx - WIDE, WIDE)],
        fields.at[0, :, pl.ds(0, PAD)],
        fields.at[0, :, pl.ds(gy - PAD, PAD)],
    )
    give_v = (
        fields.at[1, pl.ds(0, REACH)],
        fields.at[1, pl.ds(gx - REACH, REACH)],
        fields.at[2, :, pl.ds(0, PAD)],
        fields.at[2, :, pl.ds(gy - PAD, PAD)],
    )

    def rim(ref):
        return (
            ref.at[pl.ds(0, WIDE), y_core],
            ref.at[pl.ds(WIDE + gx, WIDE), y_core],
            ref.at[x_core, pl.ds(0, PAD)],
            ref.at[x_core, pl.ds(PAD + gy, PAD)],
        )

    rim_a = rim(pa)
    rim_b = rim(pb)
    rim_v = (
        us.at[pl.ds(0, REACH)],
        us.at[pl.ds(REACH + gx, REACH)],
        vs.at[:, pl.ds(0, PAD)],
        vs.at[:, pl.ds(PAD + gy, PAD)],
    )

    raw = []
    for s in range(4):
        raw.append((
            remote(cells_in.at[0], passed_cells.at[back[s]], raw_send.at[s], raw_recv.at[s], to[s]),
            remote(give_p[s], rim_a[back[s]], raw_send.at[4 + s], raw_recv.at[4 + s], to[s]),
            remote(give_v[s], rim_v[back[s]], raw_send.at[8 + s], raw_recv.at[8 + s], to[s]),
        ))

    def landed(src, dst, recv, s):
        return remote(src, dst, raw_send.at[s], recv, to[s % 4])

    loads = [
        pltpu.make_async_copy(fields.at[0], pa.at[x_core, y_core], load_sem.at[0]),
        pltpu.make_async_copy(fields.at[1], us.at[pl.ds(REACH, gx)], load_sem.at[1]),
        pltpu.make_async_copy(fields.at[2], vs.at[:, y_core], load_sem.at[2]),
        pltpu.make_async_copy(fields.at[3], ws, load_sem.at[3]),
    ]
    for copy in loads:
        copy.start()

    for s in range(4):
        @pl.when(jnp.logical_not(has[s]))
        def _(s=s):
            rim_a[s][...] = jnp.zeros(rim_a[s].shape, F32)
            rim_b[s][...] = jnp.zeros(rim_b[s].shape, F32)
            rim_v[s][...] = jnp.zeros(rim_v[s].shape, F32)

    scaled = [DT * w for w in WEIGHTS]
    source = lax.broadcasted_iota(jnp.int32, (gz, 2 * gz), 0)
    column = lax.broadcasted_iota(jnp.int32, (gz, 2 * gz), 1)
    difference = jnp.zeros((gz, 2 * gz), F32)
    for j, w in enumerate(scaled, 1):
        difference = jnp.where(jnp.logical_and(column < gz, source - column == j), w, difference)
        difference = jnp.where(jnp.logical_and(column < gz, column - source == j), -w, difference)
        difference = jnp.where(jnp.logical_and(column >= gz, source + column - gz + 1 == j), -w, difference)
    coarse = difference.astype(BF)
    zmat[0:gz, :] = coarse
    zmat[gz:2 * gz, :] = coarse
    zmat[2 * gz:, :] = (difference - coarse.astype(F32)).astype(BF)

    for copy in fetched:
        copy.wait()
    ground_t = ground[...].astype(F32).T
    for x in range(gx):
        flags[x] = jnp.broadcast_to(ground_t[:, x:x + 1], (gy, gz))

    def greet_and_send():
        pl.semaphore_wait(barrier, nby - 1 + nbx - 1)
        for s in range(4):
            @pl.when(has[s])
            def _(s=s):
                for copy in raw[s]:
                    copy.start()


    panel_part(nbx, nby, obs, slots, fracs, owners, pts, nrm, src, packet, eo, ep, feat, pieces, base,
               hot_own, greet_and_send)
    firsts = []
    for i in range(1, nby):
        peer = lax.rem(by + i, nby)
        rows = pl.ds(pl.multiple_of(peer * nbx, nbx), nbx)
        copy = remote(packet.at[rows, :], gathered.at[i], one_send.at[i], one_recv.at[i], (bx, peer))
        copy.start()
        firsts.append(copy)

    def fill(ref, rows, row_id):
        step = min(256, rows)

        def go(i, carry):
            r0 = pl.multiple_of(i * step, step)
            ids = lax.broadcasted_iota(jnp.int32, (step, 1), 0) + r0
            for b in range(nbx):
                ref[pl.ds(r0, step), b * 128:(b + 1) * 128] = jnp.where(
                    ids == row_id[b:b + 1, :], 1.0, 0.0
                ).astype(BF)
            return carry

        lax.fori_loop(0, rows // step, go, 0)

    fill(hot_own, gx * gy, cells[...] // gz)

    for copy in firsts:
        copy.wait_recv()
    mine = pl.ds(pl.multiple_of(by * nbx, nbx), nbx)
    total = packet[mine, :]
    for i in range(1, nby):
        total = total + gathered[i]
    for i in range(nbx):
        agg[i] = total[i:i + 1, :]
    seconds = []
    for i in range(1, nbx):
        peer = lax.rem(bx + i, nbx)
        copy = remote(agg.at[peer], arrived.at[bx], two_send.at[i], two_recv.at[i], (peer, by))
        copy.start()
        seconds.append(copy)
    arrived[bx] = agg[bx]

    for s in range(4):
        @pl.when(has[s])
        def _(s=s):
            landed(cells_in.at[0], passed_cells.at[s], raw_recv.at[back[s]], s).wait_recv()
            row_id = passed_cells[s] // gz
            if s == 0:
                fill(hot_lr.at[0], WIDE * gy, row_id - (gx - WIDE) * gy)
            elif s == 1:
                fill(hot_lr.at[1], WIDE * gy, row_id)
            else:
                y = row_id % gy - (gy - PAD if s == 2 else 0)
                inside = jnp.logical_and(y >= 0, y < PAD)
                fill(hot_du.at[s - 2], gx * PAD, jnp.where(inside, row_id // gy * PAD + y, -1))

    heights = lax.broadcasted_iota(jnp.int32, (gz, 1), 0)

    def targets(bt, values, cell_rows):
        for b in range(nbx):
            v = values(b)
            at = heights == cell_rows[b:b + 1, :] % gz
            hi = v.astype(BF).astype(F32)
            bt[0:gz, b * 128:(b + 1) * 128] = jnp.where(at, hi, 0.0).astype(BF)
            bt[gz:2 * gz, b * 128:(b + 1) * 128] = jnp.where(at, v - hi, 0.0).astype(BF)

    def added(hot, bt):
        both = dot_nt(hot, bt[...])
        return both[:, :gz] + both[:, gz:]

    for copy in seconds:
        copy.wait_recv()
    handed = [
        remote(arrived, passed.at[back[s]], nb_send.at[s], nb_recv.at[s], to[s]) for s in range(4)
    ]
    for s in range(4):
        @pl.when(has[s])
        def _(s=s):
            handed[s].start()

    own, theirs = bt.at[0], bt.at[1]
    targets(own, lambda b: arrived[b], cells[...])
    loads[0].wait()
    planes = min(4, gx)
    ends = 2
    near = min(2 * WIDE, gx // 2)

    def inject_own(lo, hi):
        count = hi - lo
        step = next(n for n in (6, 4, 2, 1) if count % n == 0)

        def go(i, carry):
            x = lo + i * step
            rows = pl.ds(pl.multiple_of(x * gy, gy), step * gy)
            pa[pl.ds(WIDE + x, step), PAD:PAD + gy, :] += added(hot_own[rows, :], own).reshape(step, gy, gz)
            return carry

        lax.fori_loop(0, count // step, go, 0)

    inject_own(0, near)
    inject_own(gx - near, gx)

    for s in range(4):
        @pl.when(has[s])
        def _(s=s):
            landed(give_p[s], rim_a[s], raw_recv.at[4 + back[s]], 4 + s).wait_recv()
            landed(give_v[s], rim_v[s], raw_recv.at[8 + back[s]], 8 + s).wait_recv()
            remote(arrived, passed.at[s], nb_send.at[s], nb_recv.at[back[s]], to[s]).wait_recv()
            targets(theirs, lambda b: passed[s, b], passed_cells[s])
            if s < 2:
                x0 = 0 if s == 0 else WIDE + gx
                pa[x0:x0 + WIDE, PAD:PAD + gy, :] += added(hot_lr[s], theirs).reshape(WIDE, gy, gz)
            else:
                y0 = 0 if s == 2 else PAD + gy
                pa[WIDE:WIDE + gx, y0:y0 + PAD, :] += added(hot_du[s - 2], theirs).reshape(gx, PAD, gz)

    for copy in loads[1:]:
        copy.wait()

    def z_term(f, flag):
        high = f.astype(BF)
        low = (f - high.astype(F32)).astype(BF)
        both = dot(jnp.concatenate([high, low, high], axis=1), zmat[...])
        return both[:, :gz] + flag * both[:, gz:]

    def span(get):
        total = None
        for j, w in enumerate(scaled, 1):
            term = w * (get(j) - get(-j))
            total = term if total is None else total + term
        return total

    def loop(lo, hi, step):
        def go(i, carry):
            step(i)
            return carry

        lax.fori_loop(lo, hi, go, 0, unroll=2 if (hi - lo) % 2 == 0 else 1)

    def u_plane(p, i):
        us[i] = us[i] - span(lambda j: p[i + REACH + j, PAD:PAD + gy, :])

    def v_rows(p, x, lo, hi):
        vs[x, lo:hi, :] = vs[x, lo:hi, :] - span(lambda j: p[x + WIDE, lo + j:hi + j, :])

    def w_planes(p, new, x, shift):
        rows = planes * gy
        shift_y = PAD if shift else 0
        f = p[pl.ds(x + WIDE, planes), PAD:PAD + gy, :].reshape(rows, gz)
        flag = flags[pl.ds(x, planes)].reshape(rows, gz)
        w = ws[pl.ds(x, planes)].reshape(rows, gz) - z_term(f, flag)
        ws[pl.ds(x, planes)] = w.reshape(planes, gy, gz)
        new[pl.ds(x + shift, planes), shift_y:shift_y + gy, :] = (f - z_term(w, -flag)).reshape(planes, gy, gz)

    def p_rows(p, x, lo, hi):
        change = span(lambda j: us[x + REACH + j, lo:hi, :])
        change = change + span(lambda j: vs[x, PAD + lo + j:PAD + hi + j, :])
        p[x + WIDE, PAD + lo:PAD + hi, :] = p[x + WIDE, PAD + lo:PAD + hi, :] - change

    def outer_u(p, s):
        lo = 0 if s == 0 else REACH + gx

        @pl.when(has[s])
        def _():
            loop(lo, lo + REACH, lambda i: u_plane(p, i))

    def outer_v(p, s, x0, x1):
        lo = PAD - REACH if s == 2 else PAD + gy

        @pl.when(has[s])
        def _():
            loop(x0, x1, lambda x: v_rows(p, x, lo, lo + REACH))

    for s in (0, 1):
        outer_u(pa, s)
    for s in (2, 3):
        outer_v(pa, s, 0, WIDE)
        outer_v(pa, s, gx - WIDE, gx)

    few = min(WIDE + REACH, gx // 2)
    loop(REACH, REACH + few, lambda i: u_plane(pa, i))
    loop(REACH + gx - few, REACH + gx, lambda i: u_plane(pa, i))
    loop(0, WIDE, lambda x: v_rows(pa, x, PAD, PAD + gy))
    loop(gx - WIDE, gx, lambda x: v_rows(pa, x, PAD, PAD + gy))
    third = gx // planes - 2 * ends

    def w_blocks(p, new, lo, hi, shift):
        loop(lo, hi, lambda i: w_planes(p, new, i * planes, shift))

    w_blocks(pa, pb, 0, ends, WIDE)
    w_blocks(pa, pb, ends + third, 2 * ends + third, WIDE)

    give_b = (
        pb.at[pl.ds(WIDE, WIDE), y_core],
        pb.at[pl.ds(gx, WIDE), y_core],
        pb.at[x_core, pl.ds(PAD, PAD)],
        pb.at[x_core, pl.ds(gy, PAD)],
    )
    second_rim = [
        remote(give_b[s], rim_b[back[s]], rim_send.at[s], rim_recv.at[s], to[s]) for s in range(4)
    ]

    def send_rim(s):
        @pl.when(has[s])
        def _():
            second_rim[s].start()

    loop(0, WIDE, lambda x: p_rows(pb, x, 0, gy))
    send_rim(0)
    loop(gx - WIDE, gx, lambda x: p_rows(pb, x, 0, gy))
    send_rim(1)
    if gx > 2 * near:
        inject_own(near, gx - near)
    for s in (2, 3):
        outer_v(pa, s, WIDE, gx - WIDE)
    loop(WIDE, gx - WIDE, lambda x: v_rows(pa, x, PAD, PAD + gy))
    w_blocks(pa, pb, ends, ends + third, WIDE)
    loop(REACH + few, REACH + gx - few, lambda i: u_plane(pa, i))

    def edges(x):
        p_rows(pb, x, 0, PAD)
        p_rows(pb, x, gy - PAD, gy)

    loop(WIDE, gx - WIDE, edges)
    send_rim(2)
    send_rim(3)
    loop(WIDE, gx - WIDE, lambda x: p_rows(pb, x, PAD, gy - PAD))

    w_blocks(pb, pz, 0, gx // planes, 0)
    loop(0, gx, lambda x: v_rows(pb, x, 2 * PAD, gy))
    loop(2 * REACH, gx, lambda i: u_plane(pb, i))
    for s in range(4):
        @pl.when(has[s])
        def _(s=s):
            remote(give_b[s], rim_b[s], rim_send.at[s], rim_recv.at[back[s]], to[s]).wait_recv()
    for s in (0, 1):
        outer_u(pb, s)
    loop(REACH, 2 * REACH, lambda i: u_plane(pb, i))
    loop(gx, gx + REACH, lambda i: u_plane(pb, i))
    for s in (2, 3):
        outer_v(pb, s, 0, gx)

    def outer_rows(x):
        v_rows(pb, x, PAD, 2 * PAD)
        v_rows(pb, x, gy, gy + PAD)

    loop(0, gx, outer_rows)

    for copy in firsts + seconds:
        copy.wait_send()
    for s in range(4):
        @pl.when(has[s])
        def _(s=s):
            for copy in raw[s]:
                copy.wait_send()
            handed[s].wait_send()
            second_rim[s].wait_send()


def last_kernel(pz, us, vs, ws, out, held, sems):
    gx, gy, gz = ws.shape
    step = min(8, gx)
    copies = [
        pltpu.make_async_copy(us.at[pl.ds(REACH, gx)], out.at[1], sems.at[0]),
        pltpu.make_async_copy(vs.at[:, pl.ds(PAD, gy)], out.at[2], sems.at[1]),
        pltpu.make_async_copy(ws, out.at[3], sems.at[2]),
    ]
    for copy in copies:
        copy.start()
    for part in range(gx // step):
        def plane(i, carry):
            x = part * step + i
            change = None
            for j, w in enumerate(WEIGHTS, 1):
                term = (DT * w) * (
                    us[x + REACH + j] - us[x + REACH - j]
                    + (vs[x, PAD + j:PAD + gy + j, :] - vs[x, PAD - j:PAD + gy - j, :])
                )
                change = term if change is None else change + term
            held[x] = pz[x] - change
            return carry

        lax.fori_loop(0, step, plane, 0)
        rows = pl.ds(part * step, step)
        copy = pltpu.make_async_copy(held.at[rows], out.at[0, rows], sems.at[3 + part])
        copy.start()
        copies.append(copy)
    for copy in copies:
        copy.wait()


def vmem():
    return pl.BlockSpec(memory_space=pltpu.VMEM)


def anywhere():
    return pl.BlockSpec(memory_space=pl.ANY)


def body(nbx, nby, fields, ground, observers, slots, fractions, owners, arrival_cell, panel_points, panel_normals,
         sources):
    devices = nbx * nby
    m = observers.shape[1]
    q = panel_points.shape[1]
    gx, gy, gz = fields.shape[1:]
    k = nbx * 128
    dma = pltpu.SemaphoreType.DMA
    wide = (gx + 2 * WIDE, gy + 2 * PAD, gz)
    kept = ((gx, gy, gz), (gx + 2 * REACH, gy, gz), (gx, gy + 2 * PAD, gz), (gx, gy, gz))
    sems = (9, 4, 12, 12, nby, nby, nbx, nbx, 4, 4, 4, 4)
    state = pl.pallas_call(
        functools.partial(box_kernel, nbx, nby),
        out_shape=[jax.ShapeDtypeStruct(shape, F32) for shape in kept],
        in_specs=[pl.BlockSpec(memory_space=pltpu.HBM)] * 10,
        out_specs=[vmem()] * 4,
        scratch_shapes=[
            pltpu.VMEM(wide, F32),
            pltpu.VMEM(wide, F32),
            pltpu.VMEM((gx, gy, gz), F32),
            pltpu.VMEM((3 * gz, 2 * gz), BF),
            pltpu.VMEM((gx * gy, k), BF),
            pltpu.VMEM((2, WIDE * gy, k), BF),
            pltpu.VMEM((2, gx * PAD, k), BF),
            pltpu.VMEM((2, 2 * gz, k), BF),
            pltpu.VMEM((nby, nbx, 128), F32),
            pltpu.VMEM((nbx, 1, 128), F32),
            pltpu.VMEM((nbx, 1, 128), F32),
            pltpu.VMEM((4, nbx, 1, 128), F32),
            pltpu.VMEM((4, nbx, 128), jnp.int32),
            pltpu.VMEM((3, m), F32),
            pltpu.VMEM((1, m), jnp.int32),
            pltpu.VMEM((1, m), F32),
            pltpu.VMEM((1, m), jnp.int32),
            pltpu.VMEM((3, q), F32),
            pltpu.VMEM((3, q), F32),
            pltpu.VMEM((3, sources.shape[2], q), BF),
            pltpu.VMEM((nbx, 128), jnp.int32),
            pltpu.VMEM((gx, gy), jnp.int32),
            pltpu.VMEM((devices, 128), F32),
        ] + panel_scratch(m, q, devices) + [dma((n,)) for n in sems],
        compiler_params=pltpu.CompilerParams(
            collective_id=0, has_side_effects=True, vmem_limit_bytes=44 << 20
        ),
        name="box",
    )(*[pltpu.with_memory_space_constraint(v, pltpu.HBM) for v in (
        observers,
        slots.reshape(1, m),
        fractions.reshape(1, m),
        owners.reshape(1, m),
        panel_points,
        panel_normals,
        sources.transpose(0, 2, 1),
        arrival_cell,
        ground,
        fields,
    )])
    return pl.pallas_call(
        last_kernel,
        out_shape=jax.ShapeDtypeStruct(fields.shape, F32),
        in_specs=[vmem()] * 4,
        out_specs=anywhere(),
        scratch_shapes=[pltpu.VMEM((gx, gy, gz), F32), dma((3 + gx // min(8, gx),))],
        compiler_params=pltpu.CompilerParams(vmem_limit_bytes=8 << 20),
        name="last",
    )(*state)


def solution(mesh):
    placed = (
        P(None, "bx", "by", None),
        P("bx", "by"),
        P(None, "bx"),
        P("bx"),
        P("bx"),
        P("bx", None),
        P(("bx", "by"), None, None),
        P(None, "by"),
        P(None, "by"),
        P(None, "by", None),
    )
    return jax.shard_map(
        functools.partial(body, mesh.shape["bx"], mesh.shape["by"]),
        mesh=mesh,
        in_specs=placed,
        out_specs=P(None, "bx", "by", None),
        check_vma=False,
    )
```

```python
import functools

import jax
import jax.numpy as jnp
from jax import lax
from jax.experimental import pallas as pl
from jax.experimental.pallas import tpu as pltpu
from jax.sharding import PartitionSpec as P

BF = jnp.bfloat16
F32 = jnp.float32
MESH = pl.DeviceIdType.MESH
WEIGHTS = (0.770882380518, -0.166705904415, 0.02084314277)
DT = 0.5
SOFTENING = 0.01
REACH = 3
WIDE = 6
PAD = 8
FEATURES = 80


def split3(x):
    a = x.astype(BF).astype(F32)
    r = x - a
    b = r.astype(BF).astype(F32)
    return a, b, r - b


def dot(a, b):
    return jnp.dot(a, b, preferred_element_type=F32)


def dot_nt(a, b):
    return lax.dot_general(a, b, (((1,), (1,)), ((), ())), preferred_element_type=F32)


def panel_scratch(m, q, devices):
    return [
        pltpu.VMEM((8, m), F32),
        pltpu.VMEM((8, q), F32),
        pltpu.VMEM((2, q, FEATURES), BF),
        pltpu.VMEM((3 * devices, 128), F32),
        pltpu.VMEM((devices, 128), F32),
    ]


def panel_part(nbx, nby, obs, slots, fracs, owners, pts, nrm, src, packet, eo, ep, feat, pieces, base, kern, ready):
    m = obs.shape[1]
    q = pts.shape[1]
    samples = src.shape[1]
    devices = nbx * nby
    tile = min(1024, m, kern.shape[1])
    chunk = min(512, q)
    sub = 256
    block = 256

    o = obs[...]
    eo[0:3, :] = o
    eo[3:4, :] = jnp.sum(o * o, axis=0, keepdims=True)
    eo[4:5, :] = jnp.ones((1, m), F32)
    eo[5:8, :] = jnp.zeros((3, m), F32)
    p = pts[...]
    n = nrm[...]

    def lay(k):
        s = split3(ep[...])
        rows = [s[0], s[1], s[2]] * 3 + [jnp.zeros_like(s[0])]
        table = jnp.concatenate(rows + [jnp.zeros((128 - FEATURES, q), F32)], axis=0)
        feat[k] = table.T[:, :FEATURES].astype(BF)

    ep[0:3, :] = -2.0 * p
    ep[3:4, :] = jnp.ones((1, q), F32)
    ep[4:5, :] = jnp.sum(p * p, axis=0, keepdims=True) + SOFTENING
    ep[5:8, :] = jnp.zeros((3, q), F32)
    lay(0)
    ep[0:3, :] = n
    ep[3:4, :] = jnp.zeros((1, q), F32)
    ep[4:5, :] = -jnp.sum(p * n, axis=0, keepdims=True)
    lay(1)
    ready()
    pieces[...] = jnp.zeros_like(pieces)
    base[...] = jnp.zeros_like(base)
    row = lax.broadcasted_iota(jnp.int32, (devices, 1), 0)
    row_owner = (row % nbx) * nby + row // nbx
    before = (
        lax.broadcasted_iota(jnp.int32, (sub, sub), 0) < lax.broadcasted_iota(jnp.int32, (sub, sub), 1)
    ).astype(F32).astype(BF)
    ranks = lax.broadcasted_iota(jnp.int32, (128, 1), 0).astype(F32)
    times = lax.broadcasted_iota(jnp.int32, (samples, 1), 0)

    def one_tile(t, carry):
        o0 = pl.multiple_of(t * tile, tile)
        here = pl.ds(o0, tile)
        e = split3(eo[:, here])
        of = jnp.concatenate(
            [e[0]] * 3 + [e[1]] * 3 + [e[2]] * 3 + [jnp.zeros_like(e[0])], axis=0
        ).astype(BF)

        def one_chunk(c, acc):
            q0 = pl.multiple_of(c * chunk, chunk)
            rows = pl.ds(q0, chunk)
            for l in range(0, tile, block):
                wide = slice(l, l + block)
                for r in range(0, chunk, block):
                    some = pl.ds(q0 + r, block)
                    inverse = lax.rsqrt(dot(feat[0, some, :], of[:, wide]))
                    near = dot(feat[1, some, :], of[:, wide]) * inverse * inverse
                    kern[r:r + block, wide] = inverse.astype(BF)
                    kern[chunk + r:chunk + r + block, wide] = near.astype(BF)
                    kern[2 * chunk + r:2 * chunk + r + block, wide] = (near * inverse).astype(BF)
            for k in range(3):
                acc = acc + dot(src[k, :, rows], kern[k * chunk:(k + 1) * chunk, 0:tile])
            return acc

        history = lax.fori_loop(0, q // chunk, one_chunk, jnp.zeros((samples, tile), F32))
        slot = slots[:, here]
        frac = fracs[:, here]
        weights = jnp.where(times == slot, 1.0 - frac, 0.0) + jnp.where(times == slot + 1, frac, 0.0)
        value = jnp.sum(history * weights, axis=0, keepdims=True)
        parts = split3(value)
        owner = owners[:, here]
        mine = owner == row_owner
        hot = jnp.where(mine, 1.0, 0.0)
        seen = base[...]
        ranks_here = []
        for s in range(tile // sub):
            part = hot[:, s * sub:(s + 1) * sub]
            earlier = dot(part.astype(BF), before) + seen[:, 0:1]
            ranks_here.append(jnp.sum(part * earlier, axis=0, keepdims=True))
            seen = seen + jnp.sum(part, axis=1, keepdims=True)
        base[...] = seen
        rank = jnp.concatenate(ranks_here, axis=1)
        at_rank = jnp.where(rank == ranks, 1.0, 0.0).astype(BF)
        loads = jnp.concatenate([jnp.where(mine, v, 0.0) for v in parts], axis=0).astype(BF)
        pieces[...] += dot_nt(loads, at_rank)
        return carry

    lax.fori_loop(0, m // tile, one_tile, 0)
    packet[...] = pieces[0:devices, :] + pieces[devices:2 * devices, :] + pieces[2 * devices:, :]


def box_kernel(nbx, nby, obs_in, slots_in, fracs_in, owners_in, pts_in, nrm_in, src_in, cells_in, ground_in, fields,
               pz, us, vs, ws, pa, pb, flags, zmat, hot_own, hot_lr, hot_du, bt,
               gathered, agg, arrived, passed, passed_cells, obs, slots, fracs, owners, pts, nrm, src, cells, ground,
               packet, eo, ep, feat, pieces, base, in_sem, load_sem, raw_send, raw_recv, one_send, one_recv,
               two_send, two_recv, nb_send, nb_recv, rim_send, rim_recv):
    bx = lax.axis_index("bx")
    by = lax.axis_index("by")
    gx, gy, gz = fields.shape[1:]
    arrivals = nbx * 128
    has = (bx > 0, bx < nbx - 1, by > 0, by < nby - 1)
    to = (
        (jnp.maximum(bx - 1, 0), by),
        (jnp.minimum(bx + 1, nbx - 1), by),
        (bx, jnp.maximum(by - 1, 0)),
        (bx, jnp.minimum(by + 1, nby - 1)),
    )
    back = (1, 0, 3, 2)

    fetched = [
        pltpu.make_async_copy(a, b, in_sem.at[i])
        for i, (a, b) in enumerate((
            (cells_in.at[0], cells), (ground_in, ground), (src_in, src), (obs_in, obs), (slots_in, slots),
            (fracs_in, fracs), (owners_in, owners), (pts_in, pts), (nrm_in, nrm),
        ))
    ]
    for copy in fetched:
        copy.start()
    barrier = pltpu.get_barrier_semaphore()
    for i in range(1, nby):
        pl.semaphore_signal(barrier, inc=1, device_id=(bx, lax.rem(by + i, nby)), device_id_type=MESH)
    for i in range(1, nbx):
        pl.semaphore_signal(barrier, inc=1, device_id=(lax.rem(bx + i, nbx), by), device_id_type=MESH)

    def remote(src, dst, send, recv, target):
        return pltpu.make_async_remote_copy(
            src_ref=src, dst_ref=dst, send_sem=send, recv_sem=recv, device_id=target, device_id_type=MESH
        )

    x_core = pl.ds(WIDE, gx)
    y_core = pl.ds(PAD, gy)
    give_p = (
        fields.at[0, pl.ds(0, WIDE)],
        fields.at[0, pl.ds(gx - WIDE, WIDE)],
        fields.at[0, :, pl.ds(0, PAD)],
        fields.at[0, :, pl.ds(gy - PAD, PAD)],
    )
    give_v = (
        fields.at[1, pl.ds(0, REACH)],
        fields.at[1, pl.ds(gx - REACH, REACH)],
        fields.at[2, :, pl.ds(0, PAD)],
        fields.at[2, :, pl.ds(gy - PAD, PAD)],
    )

    def rim(ref):
        return (
            ref.at[pl.ds(0, WIDE), y_core],
            ref.at[pl.ds(WIDE + gx, WIDE), y_core],
            ref.at[x_core, pl.ds(0, PAD)],
            ref.at[x_core, pl.ds(PAD + gy, PAD)],
        )

    rim_a = rim(pa)
    rim_b = rim(pb)
    rim_v = (
        us.at[pl.ds(0, REACH)],
        us.at[pl.ds(REACH + gx, REACH)],
        vs.at[:, pl.ds(0, PAD)],
        vs.at[:, pl.ds(PAD + gy, PAD)],
    )

    raw = []
    for s in range(4):
        raw.append((
            remote(cells_in.at[0], passed_cells.at[back[s]], raw_send.at[s], raw_recv.at[s], to[s]),
            remote(give_p[s], rim_a[back[s]], raw_send.at[4 + s], raw_recv.at[4 + s], to[s]),
            remote(give_v[s], rim_v[back[s]], raw_send.at[8 + s], raw_recv.at[8 + s], to[s]),
        ))

    def landed(src, dst, recv, s):
        return remote(src, dst, raw_send.at[s], recv, to[s % 4])

    loads = [
        pltpu.make_async_copy(fields.at[0], pa.at[x_core, y_core], load_sem.at[0]),
        pltpu.make_async_copy(fields.at[1], us.at[pl.ds(REACH, gx)], load_sem.at[1]),
        pltpu.make_async_copy(fields.at[2], vs.at[:, y_core], load_sem.at[2]),
        pltpu.make_async_copy(fields.at[3], ws, load_sem.at[3]),
    ]
    for copy in loads:
        copy.start()

    for s in range(4):
        @pl.when(jnp.logical_not(has[s]))
        def _(s=s):
            rim_a[s][...] = jnp.zeros(rim_a[s].shape, F32)
            rim_b[s][...] = jnp.zeros(rim_b[s].shape, F32)
            rim_v[s][...] = jnp.zeros(rim_v[s].shape, F32)

    scaled = [DT * w for w in WEIGHTS]
    source = lax.broadcasted_iota(jnp.int32, (gz, 2 * gz), 0)
    column = lax.broadcasted_iota(jnp.int32, (gz, 2 * gz), 1)
    difference = jnp.zeros((gz, 2 * gz), F32)
    for j, w in enumerate(scaled, 1):
        difference = jnp.where(jnp.logical_and(column < gz, source - column == j), w, difference)
        difference = jnp.where(jnp.logical_and(column < gz, column - source == j), -w, difference)
        difference = jnp.where(jnp.logical_and(column >= gz, source + column - gz + 1 == j), -w, difference)
    coarse = difference.astype(BF)
    zmat[0:gz, :] = coarse
    zmat[gz:2 * gz, :] = coarse
    zmat[2 * gz:, :] = (difference - coarse.astype(F32)).astype(BF)

    for copy in fetched:
        copy.wait()
    ground_t = ground[...].astype(F32).T
    for x in range(gx):
        flags[x] = jnp.broadcast_to(ground_t[:, x:x + 1], (gy, gz))

    def greet_and_send():
        pl.semaphore_wait(barrier, nby - 1 + nbx - 1)
        for s in range(4):
            @pl.when(has[s])
            def _(s=s):
                for copy in raw[s]:
                    copy.start()


    panel_part(nbx, nby, obs, slots, fracs, owners, pts, nrm, src, packet, eo, ep, feat, pieces, base,
               hot_own, greet_and_send)
    firsts = []
    for i in range(1, nby):
        peer = lax.rem(by + i, nby)
        rows = pl.ds(pl.multiple_of(peer * nbx, nbx), nbx)
        copy = remote(packet.at[rows, :], gathered.at[i], one_send.at[i], one_recv.at[i], (bx, peer))
        copy.start()
        firsts.append(copy)

    def fill(ref, rows, row_id):
        step = min(256, rows)

        def go(i, carry):
            r0 = pl.multiple_of(i * step, step)
            ids = lax.broadcasted_iota(jnp.int32, (step, 1), 0) + r0
            for b in range(nbx):
                ref[pl.ds(r0, step), b * 128:(b + 1) * 128] = jnp.where(
                    ids == row_id[b:b + 1, :], 1.0, 0.0
                ).astype(BF)
            return carry

        lax.fori_loop(0, rows // step, go, 0)

    fill(hot_own, gx * gy, cells[...] // gz)

    for copy in firsts:
        copy.wait_recv()
    mine = pl.ds(pl.multiple_of(by * nbx, nbx), nbx)
    total = packet[mine, :]
    for i in range(1, nby):
        total = total + gathered[i]
    for i in range(nbx):
        agg[i] = total[i:i + 1, :]
    seconds = []
    for i in range(1, nbx):
        peer = lax.rem(bx + i, nbx)
        copy = remote(agg.at[peer], arrived.at[bx], two_send.at[i], two_recv.at[i], (peer, by))
        copy.start()
        seconds.append(copy)
    arrived[bx] = agg[bx]

    for s in range(4):
        @pl.when(has[s])
        def _(s=s):
            landed(cells_in.at[0], passed_cells.at[s], raw_recv.at[back[s]], s).wait_recv()
            row_id = passed_cells[s] // gz
            if s == 0:
                fill(hot_lr.at[0], WIDE * gy, row_id - (gx - WIDE) * gy)
            elif s == 1:
                fill(hot_lr.at[1], WIDE * gy, row_id)
            else:
                y = row_id % gy - (gy - PAD if s == 2 else 0)
                inside = jnp.logical_and(y >= 0, y < PAD)
                fill(hot_du.at[s - 2], gx * PAD, jnp.where(inside, row_id // gy * PAD + y, -1))

    heights = lax.broadcasted_iota(jnp.int32, (gz, 1), 0)

    def targets(bt, values, cell_rows):
        for b in range(nbx):
            v = values(b)
            at = heights == cell_rows[b:b + 1, :] % gz
            hi = v.astype(BF).astype(F32)
            bt[0:gz, b * 128:(b + 1) * 128] = jnp.where(at, hi, 0.0).astype(BF)
            bt[gz:2 * gz, b * 128:(b + 1) * 128] = jnp.where(at, v - hi, 0.0).astype(BF)

    def added(hot, bt):
        both = dot_nt(hot, bt[...])
        return both[:, :gz] + both[:, gz:]

    for copy in seconds:
        copy.wait_recv()
    handed = [
        remote(arrived, passed.at[back[s]], nb_send.at[s], nb_recv.at[s], to[s]) for s in range(4)
    ]
    for s in range(4):
        @pl.when(has[s])
        def _(s=s):
            handed[s].start()

    own, theirs = bt.at[0], bt.at[1]
    targets(own, lambda b: arrived[b], cells[...])
    loads[0].wait()
    planes = min(4, gx)
    ends = 2
    near = min(2 * WIDE, gx // 2)

    def inject_own(lo, hi):
        count = hi - lo
        step = next(n for n in (6, 4, 2, 1) if count % n == 0)

        def go(i, carry):
            x = lo + i * step
            rows = pl.ds(pl.multiple_of(x * gy, gy), step * gy)
            pa[pl.ds(WIDE + x, step), PAD:PAD + gy, :] += added(hot_own[rows, :], own).reshape(step, gy, gz)
            return carry

        lax.fori_loop(0, count // step, go, 0)

    inject_own(0, near)
    inject_own(gx - near, gx)

    for s in range(4):
        @pl.when(has[s])
        def _(s=s):
            landed(give_p[s], rim_a[s], raw_recv.at[4 + back[s]], 4 + s).wait_recv()
            landed(give_v[s], rim_v[s], raw_recv.at[8 + back[s]], 8 + s).wait_recv()
            remote(arrived, passed.at[s], nb_send.at[s], nb_recv.at[back[s]], to[s]).wait_recv()
            targets(theirs, lambda b: passed[s, b], passed_cells[s])
            if s < 2:
                x0 = 0 if s == 0 else WIDE + gx
                pa[x0:x0 + WIDE, PAD:PAD + gy, :] += added(hot_lr[s], theirs).reshape(WIDE, gy, gz)
            else:
                y0 = 0 if s == 2 else PAD + gy
                pa[WIDE:WIDE + gx, y0:y0 + PAD, :] += added(hot_du[s - 2], theirs).reshape(gx, PAD, gz)

    for copy in loads[1:]:
        copy.wait()

    def z_term(f, flag):
        high = f.astype(BF)
        low = (f - high.astype(F32)).astype(BF)
        both = dot(jnp.concatenate([high, low, high], axis=1), zmat[...])
        return both[:, :gz] + flag * both[:, gz:]

    def span(get):
        total = None
        for j, w in enumerate(scaled, 1):
            term = w * (get(j) - get(-j))
            total = term if total is None else total + term
        return total

    def loop(lo, hi, step):
        def go(i, carry):
            step(i)
            return carry

        lax.fori_loop(lo, hi, go, 0, unroll=next(n for n in (2, 3, 1) if (hi - lo) % n == 0))

    def u_plane(p, i):
        us[i] = us[i] - span(lambda j: p[i + REACH + j, PAD:PAD + gy, :])

    def v_rows(p, x, lo, hi):
        vs[x, lo:hi, :] = vs[x, lo:hi, :] - span(lambda j: p[x + WIDE, lo + j:hi + j, :])

    def w_planes(p, new, x, shift):
        rows = planes * gy
        shift_y = PAD if shift else 0
        f = p[pl.ds(x + WIDE, planes), PAD:PAD + gy, :].reshape(rows, gz)
        flag = flags[pl.ds(x, planes)].reshape(rows, gz)
        w = ws[pl.ds(x, planes)].reshape(rows, gz) - z_term(f, flag)
        ws[pl.ds(x, planes)] = w.reshape(planes, gy, gz)
        new[pl.ds(x + shift, planes), shift_y:shift_y + gy, :] = (f - z_term(w, -flag)).reshape(planes, gy, gz)

    def p_rows(p, x, lo, hi):
        change = span(lambda j: us[x + REACH + j, lo:hi, :])
        change = change + span(lambda j: vs[x, PAD + lo + j:PAD + hi + j, :])
        p[x + WIDE, PAD + lo:PAD + hi, :] = p[x + WIDE, PAD + lo:PAD + hi, :] - change

    def outer_u(p, s):
        lo = 0 if s == 0 else REACH + gx

        @pl.when(has[s])
        def _():
            loop(lo, lo + REACH, lambda i: u_plane(p, i))

    def outer_v(p, s, x0, x1):
        lo = PAD - REACH if s == 2 else PAD + gy

        @pl.when(has[s])
        def _():
            loop(x0, x1, lambda x: v_rows(p, x, lo, lo + REACH))

    for s in (0, 1):
        outer_u(pa, s)
    for s in (2, 3):
        outer_v(pa, s, 0, WIDE)
        outer_v(pa, s, gx - WIDE, gx)

    few = min(WIDE + REACH, gx // 2)
    loop(REACH, REACH + few, lambda i: u_plane(pa, i))
    loop(REACH + gx - few, REACH + gx, lambda i: u_plane(pa, i))
    loop(0, WIDE, lambda x: v_rows(pa, x, PAD, PAD + gy))
    loop(gx - WIDE, gx, lambda x: v_rows(pa, x, PAD, PAD + gy))
    third = gx // planes - 2 * ends

    def w_blocks(p, new, lo, hi, shift):
        loop(lo, hi, lambda i: w_planes(p, new, i * planes, shift))

    w_blocks(pa, pb, 0, ends, WIDE)
    w_blocks(pa, pb, ends + third, 2 * ends + third, WIDE)

    give_b = (
        pb.at[pl.ds(WIDE, WIDE), y_core],
        pb.at[pl.ds(gx, WIDE), y_core],
        pb.at[x_core, pl.ds(PAD, PAD)],
        pb.at[x_core, pl.ds(gy, PAD)],
    )
    second_rim = [
        remote(give_b[s], rim_b[back[s]], rim_send.at[s], rim_recv.at[s], to[s]) for s in range(4)
    ]

    def send_rim(s):
        @pl.when(has[s])
        def _():
            second_rim[s].start()

    loop(0, WIDE, lambda x: p_rows(pb, x, 0, gy))
    send_rim(0)
    loop(gx - WIDE, gx, lambda x: p_rows(pb, x, 0, gy))
    send_rim(1)
    if gx > 2 * near:
        inject_own(near, gx - near)
    for s in (2, 3):
        outer_v(pa, s, WIDE, gx - WIDE)
    loop(WIDE, gx - WIDE, lambda x: v_rows(pa, x, PAD, PAD + gy))
    w_blocks(pa, pb, ends, ends + third, WIDE)
    loop(REACH + few, REACH + gx - few, lambda i: u_plane(pa, i))

    def edges(x):
        p_rows(pb, x, 0, PAD)
        p_rows(pb, x, gy - PAD, gy)

    loop(WIDE, gx - WIDE, edges)
    send_rim(2)
    send_rim(3)
    loop(WIDE, gx - WIDE, lambda x: p_rows(pb, x, PAD, gy - PAD))

    w_blocks(pb, pz, 0, gx // planes, 0)
    loop(0, gx, lambda x: v_rows(pb, x, 2 * PAD, gy))
    loop(2 * REACH, gx, lambda i: u_plane(pb, i))
    for s in range(4):
        @pl.when(has[s])
        def _(s=s):
            remote(give_b[s], rim_b[s], rim_send.at[s], rim_recv.at[back[s]], to[s]).wait_recv()
    for s in (0, 1):
        outer_u(pb, s)
    loop(REACH, 2 * REACH, lambda i: u_plane(pb, i))
    loop(gx, gx + REACH, lambda i: u_plane(pb, i))
    for s in (2, 3):
        outer_v(pb, s, 0, gx)

    def outer_rows(x):
        v_rows(pb, x, PAD, 2 * PAD)
        v_rows(pb, x, gy, gy + PAD)

    loop(0, gx, outer_rows)

    for copy in firsts + seconds:
        copy.wait_send()
    for s in range(4):
        @pl.when(has[s])
        def _(s=s):
            for copy in raw[s]:
                copy.wait_send()
            handed[s].wait_send()
            second_rim[s].wait_send()


def last_kernel(pz, us, vs, ws, out, held, sems):
    gx, gy, gz = ws.shape
    step = min(8, gx)
    copies = [
        pltpu.make_async_copy(us.at[pl.ds(REACH, gx)], out.at[1], sems.at[0]),
        pltpu.make_async_copy(vs.at[:, pl.ds(PAD, gy)], out.at[2], sems.at[1]),
        pltpu.make_async_copy(ws, out.at[3], sems.at[2]),
    ]
    for copy in copies:
        copy.start()
    for part in range(gx // step):
        def plane(i, carry):
            x = part * step + i
            change = None
            for j, w in enumerate(WEIGHTS, 1):
                term = (DT * w) * (
                    us[x + REACH + j] - us[x + REACH - j]
                    + (vs[x, PAD + j:PAD + gy + j, :] - vs[x, PAD - j:PAD + gy - j, :])
                )
                change = term if change is None else change + term
            held[x] = pz[x] - change
            return carry

        lax.fori_loop(0, step, plane, 0)
        rows = pl.ds(part * step, step)
        copy = pltpu.make_async_copy(held.at[rows], out.at[0, rows], sems.at[3 + part])
        copy.start()
        copies.append(copy)
    for copy in copies:
        copy.wait()


def vmem():
    return pl.BlockSpec(memory_space=pltpu.VMEM)


def anywhere():
    return pl.BlockSpec(memory_space=pl.ANY)


def body(nbx, nby, fields, ground, observers, slots, fractions, owners, arrival_cell, panel_points, panel_normals,
         sources):
    devices = nbx * nby
    m = observers.shape[1]
    q = panel_points.shape[1]
    gx, gy, gz = fields.shape[1:]
    k = nbx * 128
    dma = pltpu.SemaphoreType.DMA
    wide = (gx + 2 * WIDE, gy + 2 * PAD, gz)
    kept = ((gx, gy, gz), (gx + 2 * REACH, gy, gz), (gx, gy + 2 * PAD, gz), (gx, gy, gz))
    sems = (9, 4, 12, 12, nby, nby, nbx, nbx, 4, 4, 4, 4)
    state = pl.pallas_call(
        functools.partial(box_kernel, nbx, nby),
        out_shape=[jax.ShapeDtypeStruct(shape, F32) for shape in kept],
        in_specs=[pl.BlockSpec(memory_space=pltpu.HBM)] * 10,
        out_specs=[vmem()] * 4,
        scratch_shapes=[
            pltpu.VMEM(wide, F32),
            pltpu.VMEM(wide, F32),
            pltpu.VMEM((gx, gy, gz), F32),
            pltpu.VMEM((3 * gz, 2 * gz), BF),
            pltpu.VMEM((gx * gy, k), BF),
            pltpu.VMEM((2, WIDE * gy, k), BF),
            pltpu.VMEM((2, gx * PAD, k), BF),
            pltpu.VMEM((2, 2 * gz, k), BF),
            pltpu.VMEM((nby, nbx, 128), F32),
            pltpu.VMEM((nbx, 1, 128), F32),
            pltpu.VMEM((nbx, 1, 128), F32),
            pltpu.VMEM((4, nbx, 1, 128), F32),
            pltpu.VMEM((4, nbx, 128), jnp.int32),
            pltpu.VMEM((3, m), F32),
            pltpu.VMEM((1, m), jnp.int32),
            pltpu.VMEM((1, m), F32),
            pltpu.VMEM((1, m), jnp.int32),
            pltpu.VMEM((3, q), F32),
            pltpu.VMEM((3, q), F32),
            pltpu.VMEM((3, sources.shape[2], q), BF),
            pltpu.VMEM((nbx, 128), jnp.int32),
            pltpu.VMEM((gx, gy), jnp.int32),
            pltpu.VMEM((devices, 128), F32),
        ] + panel_scratch(m, q, devices) + [dma((n,)) for n in sems],
        compiler_params=pltpu.CompilerParams(
            collective_id=0, has_side_effects=True, vmem_limit_bytes=44 << 20
        ),
        name="box",
    )(*[pltpu.with_memory_space_constraint(v, pltpu.HBM) for v in (
        observers,
        slots.reshape(1, m),
        fractions.reshape(1, m),
        owners.reshape(1, m),
        panel_points,
        panel_normals,
        sources.transpose(0, 2, 1),
        arrival_cell,
        ground,
        fields,
    )])
    return pl.pallas_call(
        last_kernel,
        out_shape=jax.ShapeDtypeStruct(fields.shape, F32),
        in_specs=[vmem()] * 4,
        out_specs=anywhere(),
        scratch_shapes=[pltpu.VMEM((gx, gy, gz), F32), dma((3 + gx // min(8, gx),))],
        compiler_params=pltpu.CompilerParams(vmem_limit_bytes=8 << 20),
        name="last",
    )(*state)


def solution(mesh):
    placed = (
        P(None, "bx", "by", None),
        P("bx", "by"),
        P(None, "bx"),
        P("bx"),
        P("bx"),
        P("bx", None),
        P(("bx", "by"), None, None),
        P(None, "by"),
        P(None, "by"),
        P(None, "by", None),
    )
    return jax.shard_map(
        functools.partial(body, mesh.shape["bx"], mesh.shape["by"]),
        mesh=mesh,
        in_specs=placed,
        out_specs=P(None, "bx", "by", None),
        check_vma=False,
    )
```
